256 devices in a mesh: px: 8 (over z), py: 32 (over x, y, core).
Axes of the slice: x: 4, y: 4, z: 8, core: 2. Of those that a mesh axis runs over, the one named last changes fastest.
Arguments:
- right_side: float32 [8, 2048, 2048], P(None, 'py', 'px'), may hold values from -6 to 6
- solution_in: float32 [8, 2048, 2048], P(None, 'py', 'px'), may hold values from -4 to 4
- classes: int32 [8, 2048, 2048], P(None, 'py', 'px'), may hold values from 0 to 15
- coeff_table: float32 [16], replicated, may hold values from 0.2 to 5
- eigenvectors: bfloat16 [2048, 2048], replicated, may hold values from -0.053880558 to 0.053880558, as said below
- eigenvalues: float32 [2048], replicated, may hold values from 0.01 to 4
- level_shift: float32 [8], replicated, may hold values from 0.3 to 3
Outputs:
- solution: float32 [8, 2048, 2048], P(None, 'py', 'px')
- residual: float32 [8, 2048, 2048], P(None, 'py', 'px')
- direction: float32 [8, 2048, 2048], P(None, 'py', 'px')
The draws below stay inside these ranges and needn't reach their ends.
Inputs may be any that keep to these rules, and one draw needn't show every extreme that they name: eigenvectors is a symmetric matrix.
All inputs are finite; a program needn't handle non-finite values.
Results may differ from the reference program's by a relative error of at most 0.034.
Values may be sent and summed in bfloat16 or wider, within the bound.
A program may use at most 64 MiB of HBM per device.

```python
import math
import jax
import jax.numpy as jnp
from jax import lax

N = 2048
NZ = 8
ITERS = 2
CLASSES = 16


def draw_eigenvectors(key, part):
    index_line = jnp.arange(N, dtype=jnp.int32) + 1
    product = index_line[:, None] * index_line[None, :] % (2 * (N + 1))
    base = math.sqrt(2.0 / (N + 1)) * jnp.sin(math.pi * product.astype(jnp.float32) / (N + 1))
    noise = jnp.clip(jax.random.normal(key, (N, N), jnp.float32), -4.0, 4.0)
    symmetric = (noise + noise.T) * (0.125 / math.sqrt(N))
    return (base + symmetric).astype(jnp.bfloat16)


def touch_ends(values, rng, smallest, top_value):
    longest = values.shape.index(max(values.shape))
    spots = []
    for shift in (0, 1):
        where = [jax.random.randint(jax.random.fold_in(rng, axis), (), 0, length) for axis, length in enumerate(values.shape)]
        where[longest] = (where[longest] + shift) % values.shape[longest]
        spots.append(tuple(where))
    return values.at[spots[0]].set(smallest).at[spots[1]].set(top_value)


def levels(own_key, extent, split, smallest, largest):
    loudness, own = 1.0, jax.random.fold_in(own_key, 6)
    for position, blocks in split:
        heights = jnp.exp(jax.random.uniform(jax.random.fold_in(own, position), (blocks,), jnp.float32, smallest / len(split), largest / len(split)))
        loudness = loudness * jnp.repeat(heights, extent[position] // blocks).reshape([-1 if axis == position else 1 for axis in range(len(extent))])
    return loudness


def scatter_about(rng, dims, scale, most, shards=(), kind=jnp.bfloat16):
    values = scale * jax.random.normal(rng, dims, jnp.float32)
    if shards:
        values = values * levels(rng, dims, shards, -0.22, 0.18)
    return jnp.clip(values, -most, most).astype(kind)


def setup_inputs(seed: int = 0) -> dict:
    seeds = jax.random.split(jax.random.key(seed), 8)
    return {
        "right_side": scatter_about(seeds[0], (NZ, N, N), 1.0, 6.0, ((1, 32), (2, 8)), jnp.float32),
        "solution_in": scatter_about(seeds[1], (NZ, N, N), 0.5, 4.0, ((1, 32), (2, 8)), jnp.float32),
        "classes": touch_ends(jax.random.randint(seeds[2], (NZ, N, N), 0, CLASSES), jax.random.fold_in(seeds[2], 1), 0, CLASSES - 1).astype(jnp.int32),
        "coeff_table": jnp.clip(jnp.exp(jax.random.uniform(seeds[3], (CLASSES,), jnp.float32, math.log(0.2), math.log(5.0))), 0.2, 5.0),
        "eigenvectors": draw_eigenvectors(jax.random.fold_in(seeds[7], 71), 0),
        "eigenvalues": jnp.clip(jnp.exp(jax.random.uniform(seeds[5], (N,), jnp.float32, math.log(0.01), math.log(4.0))), 0.01, 4.0),
        "level_shift": jnp.clip(jnp.exp(jax.random.uniform(seeds[6], (NZ,), jnp.float32, math.log(0.3), math.log(3.0))), 0.3, 3.0),
    }


def apply_operator(field, coeff):
    padded = jnp.pad(field, ((0, 0), (1, 1), (1, 1)))
    coeff_pad = jnp.pad(coeff, ((0, 0), (1, 1), (1, 1)))
    height = field.shape[1]
    width = field.shape[2]
    result = jnp.zeros_like(field)
    for shift_y, shift_x in ((0, 1), (2, 1), (1, 0), (1, 2)):
        neighbour = padded[:, shift_y:shift_y + height, shift_x:shift_x + width]
        other = coeff_pad[:, shift_y:shift_y + height, shift_x:shift_x + width]
        result = result + 0.5 * (coeff + other) * (field - neighbour)
    vertical = 0.5 * (coeff[:-1] + coeff[1:]) * (field[:-1] - field[1:])
    zero_layer = jnp.zeros_like(field[:1])
    result = result + jnp.concatenate((vertical, zero_layer), 0) - jnp.concatenate((zero_layer, vertical), 0)
    return result


def precondition(residual, eigenvectors, eigenvalues, level_shift):
    basis = eigenvectors.astype(jnp.float32)
    rounded = residual.astype(jnp.bfloat16).astype(jnp.float32)
    first = jnp.einsum('kyx,xi->kyi', rounded, basis, precision=lax.Precision.HIGHEST).astype(jnp.bfloat16)
    second = jnp.einsum('kyi,yj->kji', first.astype(jnp.float32), basis, precision=lax.Precision.HIGHEST)
    denom = eigenvalues[None, :, None] + eigenvalues[None, None, :] + level_shift[:, None, None]
    scaled = (second / denom).astype(jnp.bfloat16)
    fourth = jnp.einsum('kji,yj->kyi', scaled.astype(jnp.float32), basis, precision=lax.Precision.HIGHEST).astype(jnp.bfloat16)
    return jnp.einsum('kyi,xi->kyx', fourth.astype(jnp.float32), basis, precision=lax.Precision.HIGHEST)


def reference(right_side, solution_in, classes, coeff_table, eigenvectors, eigenvalues, level_shift):
    coeff = coeff_table[classes]
    solution = solution_in
    residual = right_side - apply_operator(solution_in, coeff)
    direction = jnp.zeros_like(residual)
    gamma_prev = jnp.float32(1.0)
    for iteration in range(ITERS):
        precond = precondition(residual, eigenvectors, eigenvalues, level_shift)
        gamma = jnp.sum(residual * precond)
        if iteration == 0:
            direction = precond
        else:
            direction = precond + (gamma / gamma_prev) * direction
        image = apply_operator(direction, coeff)
        alpha = gamma / jnp.sum(direction * image)
        solution = solution + alpha * direction
        residual = residual - alpha * image
        gamma_prev = gamma
    return solution, residual, direction
```

```python
import functools

import jax
import jax.numpy as jnp
from jax import lax
from jax.experimental import pallas as pl
from jax.experimental.pallas import tpu as pltpu
from jax.sharding import PartitionSpec as P

F32 = jnp.float32
BF16 = jnp.bfloat16
ROWS = 64
HIGH = lax.Precision.HIGHEST
NT = (((1,), (1,)), ((), ()))
TN = (((0,), (0,)), ((), ()))


def kernel(
    PX,
    PY,
    b_hbm,
    x_hbm,
    cls_hbm,
    table,
    vec_hbm,
    eig,
    shift,
    sol_hbm,
    res_hbm,
    dir_hbm,
    vec,
    cls,
    sol,
    res,
    direction,
    vp_x,
    vp_0,
    vp_1,
    cp,
    halo,
    chalo,
    w_e,
    w_w,
    w_s,
    w_n,
    w_z,
    w_sum,
    image,
    xsend,
    xrecv,
    ysend,
    yrecv,
    zsend,
    zrecv,
    bsend,
    brecv,
    lhs,
    s2,
    s3,
    dinv,
    eigc,
    rsend,
    rrecv,
    csend,
    crecv,
    arx_send,
    arx,
    ary_send,
    ary,
    load_sem,
    store_sem,
    halo_send,
    halo_recv,
    a2a_send,
    a2a_recv,
    ar_send,
    ar_recv,
):
    NZ, XL, N = PX, image.shape[2], vec.shape[0]
    G = N // 256
    p, q = lax.axis_index("px"), lax.axis_index("py")

    def lane(shape):
        return lax.broadcasted_iota(jnp.int32, shape, len(shape) - 1)

    def row(shape):
        return lax.broadcasted_iota(jnp.int32, shape, len(shape) - 2)

    load_cls = pltpu.make_async_copy(cls_hbm, cls, load_sem.at[0])
    load_x = pltpu.make_async_copy(x_hbm, vp_x.at[:, 8 : 8 + ROWS, :], load_sem.at[1])
    load_b = pltpu.make_async_copy(b_hbm, res, load_sem.at[2])
    load_v = pltpu.make_async_copy(vec_hbm, vec, load_sem.at[3])
    load_cls.start()
    load_x.start()
    load_b.start()
    load_v.start()

    barrier = pltpu.get_barrier_semaphore()

    @pl.loop(1, PX)
    def _(t):
        pl.semaphore_signal(barrier, inc=1, device_id={"px": lax.rem(p + t, PX)})

    @pl.loop(1, PY)
    def _(t):
        pl.semaphore_signal(barrier, inc=1, device_id={"py": lax.rem(q + t, PY)})

    load_cls.wait()
    load_x.wait()
    pl.semaphore_wait(barrier, PX - 1 + PY - 1)

    def remote(src, dst, send, recv, where):
        return pltpu.make_async_remote_copy(
            src_ref=src, dst_ref=dst, send_sem=send, recv_sem=recv, device_id=where
        )

    def halo_copies(h):
        up = {"py": lax.rem(q + 1, PY)}
        down = {"py": lax.rem(q + PY - 1, PY)}
        right = {"px": lax.rem(p + 1, PX)}
        left = {"px": lax.rem(p + PX - 1, PX)}
        return [
            remote(rsend.at[h, 0], rrecv.at[h, 1], halo_send.at[h, 0], halo_recv.at[h, 0], down),
            remote(rsend.at[h, 1], rrecv.at[h, 0], halo_send.at[h, 1], halo_recv.at[h, 1], up),
            remote(csend.at[h], crecv.at[h, 1], halo_send.at[h, 2], halo_recv.at[h, 2], left),
            remote(csend.at[h], crecv.at[h, 0], halo_send.at[h, 3], halo_recv.at[h, 3], right),
        ]

    pick_r, pick_l = row((16, XL)), lane((16, XL))

    def pick(base, kind):
        hot = ((pick_r == base) & (pick_l == 0)) | ((pick_r == base + 1) & (pick_l == XL - 1))
        return jnp.where(hot, 1.0, 0.0).astype(kind)

    def lookup(values):
        result = jnp.zeros(values.shape, F32)
        for label in range(16):
            result = jnp.where(values == label, table[label], result)
        return result

    for k in range(NZ):
        rsend[0, 0, k : k + 1, :] = vp_x[k, 8:9, :]
        rsend[0, 1, k : k + 1, :] = vp_x[k, 7 + ROWS : 8 + ROWS, :]
        rsend[0, 0, NZ + k : NZ + k + 1, :] = cls[k, 0:1, :].astype(F32)
        rsend[0, 1, NZ + k : NZ + k + 1, :] = cls[k, ROWS - 1 : ROWS, :].astype(F32)
    x_flat = vp_x[:, 8 : 8 + ROWS, :].reshape(NZ * ROWS, XL)
    cls_flat = cls[...].reshape(NZ * ROWS, XL).astype(F32)
    csend[0] = lax.dot_general(
        pick(0, F32), x_flat, NT, precision=HIGH, preferred_element_type=F32
    ) + lax.dot_general(
        pick(2, BF16), cls_flat.astype(BF16), NT, preferred_element_type=F32
    )
    copies = halo_copies(0)
    for copy in copies:
        copy.start()

    @pl.loop(0, NZ)
    def _(k):
        cp[k, 8 : 8 + ROWS, :] = lookup(cls[k])

    group, part = q // 4, lax.rem(q, 4)
    for half in range(2):
        cols = pl.ds(pl.multiple_of(group * 256 + half * 128, 128), 128)
        eigc[...] = jnp.broadcast_to(eig[:, cols], (128, 128)).T
        mine = eigc[pl.ds(pl.multiple_of(part * 32, 32), 32), 0:1] + shift[p]
        dinv[half * 32 : half * 32 + 32, :] = 1.0 / (mine + eig[...])

    has_up = jnp.where(q > 0, 1.0, 0.0).astype(F32)
    has_down = jnp.where(q < PY - 1, 1.0, 0.0).astype(F32)
    has_left = jnp.where(p > 0, 1.0, 0.0).astype(F32)
    has_right = jnp.where(p < PX - 1, 1.0, 0.0).astype(F32)

    place_r, place_l = row((16, XL)), lane((16, XL))

    def place(base, kind):
        hot_l = (place_r == base + 1) & (place_l == 0)
        hot_r = (place_r == base) & (place_l == XL - 1)
        return jnp.where(hot_l, 1.0, 0.0).astype(kind), jnp.where(hot_r, 1.0, 0.0).astype(kind)

    def wait_all(copies):
        for copy in copies:
            copy.wait_recv()

    def fill_rows(h, vp):
        for k in range(NZ):
            vp[k, 7:8, :] = rrecv[h, 0, k : k + 1, :] * has_up
            vp[k, 8 + ROWS : 9 + ROWS, :] = rrecv[h, 1, k : k + 1, :] * has_down

    wait_all(copies)
    fill_rows(0, vp_x)
    for k in range(NZ):
        cp[k, 7:8, :] = lookup(rrecv[0, 0, NZ + k : NZ + k + 1, :]) * has_up
        cp[k, 8 + ROWS : 9 + ROWS, :] = lookup(rrecv[0, 1, NZ + k : NZ + k + 1, :]) * has_down

    def columns(left, right, base, precision, kind):
        hot_l, hot_r = place(base, kind)
        out = lax.dot_general(
            (left * has_left).astype(kind), hot_l, TN, precision=precision, preferred_element_type=F32
        ) + lax.dot_general(
            (right * has_right).astype(kind), hot_r, TN, precision=precision, preferred_element_type=F32
        )
        return out.reshape(NZ, ROWS, XL)

    halo[...] = columns(crecv[0, 0], crecv[0, 1], 0, HIGH, F32)
    chalo[...] = columns(lookup(crecv[0, 0]), lookup(crecv[0, 1]), 2, HIGH, F32)

    lanes = lane((ROWS, XL))

    def east(values, edge):
        return jnp.where(lanes == XL - 1, edge, pltpu.roll(values, XL - 1, 1))

    def west(values, edge):
        return jnp.where(lanes == 0, edge, pltpu.roll(values, 1, 1))

    w_z[0] = jnp.zeros((ROWS, XL), F32)
    w_z[NZ] = jnp.zeros((ROWS, XL), F32)

    @pl.loop(0, NZ - 1)
    def _(k):
        w_z[k + 1] = 0.5 * (cp[k, 8 : 8 + ROWS, :] + cp[k + 1, 8 : 8 + ROWS, :])

    @pl.loop(0, NZ)
    def _(k):
        here = cp[k, 8 : 8 + ROWS, :]
        edge = chalo[k]
        to_e = 0.5 * (here + east(here, edge))
        to_w = 0.5 * (here + west(here, edge))
        to_n = 0.5 * (here + cp[k, 7 : 7 + ROWS, :])
        to_s = 0.5 * (here + cp[k, 9 : 9 + ROWS, :])
        w_e[k] = to_e
        w_w[k] = to_w
        w_n[k] = to_n
        w_s[k] = to_s
        w_sum[k] = to_e + to_w + to_n + to_s + w_z[k] + w_z[k + 1]

    def operator(vp, k):
        here = vp[k, 8 : 8 + ROWS, :]
        edge = halo[k]
        below = vp[jnp.maximum(k - 1, 0), 8 : 8 + ROWS, :]
        above = vp[jnp.minimum(k + 1, NZ - 1), 8 : 8 + ROWS, :]
        out = w_sum[k] * here - w_e[k] * east(here, edge) - w_w[k] * west(here, edge)
        out = out - w_n[k] * vp[k, 7 : 7 + ROWS, :] - w_s[k] * vp[k, 9 : 9 + ROWS, :]
        return here, out - w_z[k] * below - w_z[k + 1] * above

    def fold(values):
        part = values.reshape(values.shape[0] // 8, 8, values.shape[1]).sum(0)
        out = part[:, :128]
        for c in range(128, values.shape[1], 128):
            out = out + part[:, c : c + 128]
        return out

    def send_level(it, k):
        @pl.when(k != p)
        def _():
            remote(
                xsend.at[it, k], xrecv.at[it, p], a2a_send.at[it, 0], a2a_recv.at[it, 0], {"px": k}
            ).start()

        @pl.when(k == p)
        def _():
            xrecv[it, k] = xsend[it, k]

    def await_bytes(ref, sem):
        pltpu.make_async_copy(ref, ref, sem).wait()

    half_lane = lane((32, 128)) < 64

    def forward(it, gamma_prepare):
        await_bytes(xrecv.at[it, pl.ds(0, PX - 1)], a2a_recv.at[it, 0])
        for c in range(PX):
            lhs[:, c * XL : (c + 1) * XL] = xrecv[it, c]

        @pl.loop(0, G)
        def _(t):
            g = lax.rem(q // 4 + t, G)
            tile = jnp.dot(
                lhs[...],
                vec[:, pl.ds(pl.multiple_of(g * 256, 256), 256)],
                preferred_element_type=F32,
            )
            turned = jnp.concatenate([tile[:, :128], tile[:, 128:]], axis=0).T
            ysend[it, pl.ds(pl.multiple_of(g * 4, 4), 4)] = turned.astype(BF16).reshape(4, 32, 128)
            for h in range(4):
                dest = g * 4 + h

                @pl.when(dest != q)
                def _():
                    remote(
                        ysend.at[it, dest],
                        yrecv.at[it, q],
                        a2a_send.at[it, 1],
                        a2a_recv.at[it, 1],
                        {"py": dest},
                    ).start()

                @pl.when(dest == q)
                def _():
                    yrecv[it, q] = ysend[it, dest]

        gamma_prepare()
        await_bytes(yrecv.at[it, pl.ds(0, PY - 1)], a2a_recv.at[it, 1])
        for m in range(PY // 2):
            even, odd = yrecv[it, 2 * m].astype(F32), yrecv[it, 2 * m + 1].astype(F32)
            low = jnp.where(half_lane, even, pltpu.roll(odd, 64, 1))
            high = jnp.where(half_lane, pltpu.roll(even, 64, 1), odd)
            lhs[0:32, m * 128 : (m + 1) * 128] = low.astype(BF16)
            lhs[32:64, m * 128 : (m + 1) * 128] = high.astype(BF16)

    def second(it, alpha):
        def body(t, acc):
            cols = pl.ds(pl.multiple_of(t * 256, 256), 256)
            tile = jnp.dot(lhs[...], vec[:, cols], preferred_element_type=F32)
            if it == 0:
                s2[:, cols] = tile
            else:
                tile = s2[:, cols] - alpha * tile
            scaled = (tile * dinv[:, cols]).astype(BF16)
            s3[:, cols] = scaled
            return acc + fold(tile * scaled.astype(F32))

        return lax.fori_loop(0, G, body, jnp.zeros((8, 128), F32))

    def backward(it, between):
        @pl.loop(0, G)
        def _(t):
            g = lax.rem(q // 4 + t, G)
            tile = jnp.dot(
                s3[...],
                vec[:, pl.ds(pl.multiple_of(g * 256, 256), 256)],
                preferred_element_type=F32,
            )
            for h in range(2):
                low, high = tile[0:32, h * 128 : h * 128 + 128], tile[32:64, h * 128 : h * 128 + 128]
                even = jnp.where(half_lane, low, pltpu.roll(high, 64, 1))
                odd = jnp.where(half_lane, pltpu.roll(low, 64, 1), high)
                zsend[it, g * 4 + 2 * h] = even.astype(BF16)
                zsend[it, g * 4 + 2 * h + 1] = odd.astype(BF16)
            for h in range(4):
                dest = g * 4 + h

                @pl.when(dest != q)
                def _():
                    remote(
                        zsend.at[it, dest],
                        zrecv.at[it, q],
                        a2a_send.at[it, 2],
                        a2a_recv.at[it, 2],
                        {"py": dest},
                    ).start()

                @pl.when(dest == q)
                def _():
                    zrecv[it, q] = zsend[it, dest]

        between()
        await_bytes(zrecv.at[it, pl.ds(0, PY - 1)], a2a_recv.at[it, 2])
        for g in range(G):
            turned = zrecv[it, 4 * g : 4 * g + 4].reshape(128, 128).astype(F32).T.astype(BF16)
            lhs[:, g * 256 : g * 256 + 128] = turned[0:64]
            lhs[:, g * 256 + 128 : g * 256 + 256] = turned[64:128]

        @pl.loop(1, PX + 1)
        def _(t):
            c = lax.rem(p + t, PX)
            tile = jnp.dot(
                lhs[...],
                vec[:, pl.ds(pl.multiple_of(c * XL, XL), XL)],
                preferred_element_type=F32,
            )
            bsend[it, c] = tile.astype(BF16)

            @pl.when(c != p)
            def _():
                remote(
                    bsend.at[it, c],
                    brecv.at[it, p],
                    a2a_send.at[it, 3],
                    a2a_recv.at[it, 3],
                    {"px": c},
                ).start()

            @pl.when(c == p)
            def _():
                brecv[it, p] = bsend[it, c]

    def reduce_start(a, first, second_part):
        mine = jnp.concatenate(
            [first.sum(0, keepdims=True), second_part.sum(0, keepdims=True)], axis=1
        )
        arx_send[a, 0] = mine
        arx[a, p] = mine

        @pl.loop(1, PX)
        def _(t):
            dest = lax.rem(p + t, PX)
            remote(
                arx_send.at[a, 0], arx.at[a, p], ar_send.at[a, 0], ar_recv.at[a, 0], {"px": dest}
            ).start()

    def reduce_middle(a):
        await_bytes(arx.at[a, pl.ds(0, PX - 1)], ar_recv.at[a, 0])
        mine = arx[a, 0]
        for t in range(1, PX):
            mine = mine + arx[a, t]
        ary_send[a, 0] = mine
        ary[a, q] = mine

        @pl.loop(1, PY)
        def _(t):
            dest = lax.rem(q + t, PY)
            remote(
                ary_send.at[a, 0], ary.at[a, q], ar_send.at[a, 1], ar_recv.at[a, 1], {"py": dest}
            ).start()

    def reduce_end(a):
        await_bytes(ary.at[a, pl.ds(0, PY - 1)], ar_recv.at[a, 1])
        total = ary[a, 0]
        for t in range(1, PY):
            total = total + ary[a, t]
        return (
            total[:, :128].sum(1, keepdims=True),
            total[:, 128:].sum(1, keepdims=True),
        )

    zero = jnp.zeros((8, 128), F32)

    load_b.wait()

    @pl.loop(1, NZ + 1)
    def _(t):
        k = lax.rem(p + t, NZ)
        _, out = operator(vp_x, k)
        value = res[k] - out
        res[k] = value
        xsend[0, k] = value.astype(BF16)
        send_level(0, k)

    load_v.wait()

    def direction_halo(h, vp):
        for k in range(NZ):
            rsend[h, 0, k : k + 1, :] = vp[k, 8:9, :]
            rsend[h, 1, k : k + 1, :] = vp[k, 7 + ROWS : 8 + ROWS, :]
        flat = vp[:, 8 : 8 + ROWS, :].reshape(NZ * ROWS, XL).astype(BF16)
        csend[h] = lax.dot_general(pick(0, BF16), flat, NT, preferred_element_type=F32)
        copies = halo_copies(h)
        for copy in copies:
            copy.start()
        return copies

    def direction_edges(h, vp, copies):
        wait_all(copies)
        fill_rows(h, vp)
        halo[...] = columns(crecv[h, 0], crecv[h, 1], 0, None, BF16)

    forward(0, lambda: None)
    gamma_part = second(0, None)
    backward(0, lambda: None)
    await_bytes(brecv.at[0, pl.ds(0, PX - 1)], a2a_recv.at[0, 3])

    @pl.loop(0, NZ)
    def _(k):
        vp_0[k, 8 : 8 + ROWS, :] = brecv[0, k].astype(F32)

    direction_edges(1, vp_0, direction_halo(1, vp_0))

    def first_image(t, acc):
        k = lax.rem(p + t, NZ)
        here, out = operator(vp_0, k)
        image[k] = out
        xsend[1, k] = out.astype(BF16)
        send_level(1, k)
        return acc + fold(here * out)

    curve = lax.fori_loop(1, NZ + 1, first_image, zero)
    reduce_start(0, gamma_part, curve)

    forward(1, lambda: reduce_middle(0))
    gamma0, curve0 = reduce_end(0)
    alpha0 = gamma0 / curve0
    reduce_start(1, second(1, alpha0), zero)
    backward(1, lambda: reduce_middle(1))

    @pl.loop(0, NZ)
    def _(k):
        res[k] = res[k] - alpha0 * image[k]
        sol[k] = vp_x[k, 8 : 8 + ROWS, :] + alpha0 * vp_0[k, 8 : 8 + ROWS, :]

    gamma1, _ = reduce_end(1)
    beta = gamma1 / gamma0
    await_bytes(brecv.at[1, pl.ds(0, PX - 1)], a2a_recv.at[1, 3])

    @pl.loop(0, NZ)
    def _(k):
        value = brecv[1, k].astype(F32) + beta * vp_0[k, 8 : 8 + ROWS, :]
        vp_1[k, 8 : 8 + ROWS, :] = value
        direction[k] = value

    store_d = pltpu.make_async_copy(direction, dir_hbm, store_sem.at[0])
    store_d.start()
    direction_edges(2, vp_1, direction_halo(2, vp_1))

    def second_image(k, acc):
        here, out = operator(vp_1, k)
        image[k] = out
        return acc + fold(here * out)

    reduce_start(2, lax.fori_loop(0, NZ, second_image, zero), zero)
    reduce_middle(2)
    curve1, _ = reduce_end(2)
    alpha1 = gamma1 / curve1

    @pl.loop(0, NZ)
    def _(k):
        sol[k] = sol[k] + alpha1 * direction[k]
        res[k] = res[k] - alpha1 * image[k]

    store_x = pltpu.make_async_copy(sol, sol_hbm, store_sem.at[1])
    store_r = pltpu.make_async_copy(res, res_hbm, store_sem.at[2])
    store_x.start()
    store_r.start()

    for h in range(3):
        for copy in halo_copies(h):
            copy.wait_send()
    for it in range(2):
        await_bytes(xsend.at[it, pl.ds(0, PX - 1)], a2a_send.at[it, 0])
        await_bytes(ysend.at[it, pl.ds(0, PY - 1)], a2a_send.at[it, 1])
        await_bytes(zsend.at[it, pl.ds(0, PY - 1)], a2a_send.at[it, 2])
        await_bytes(bsend.at[it, pl.ds(0, PX - 1)], a2a_send.at[it, 3])
    for a in range(3):
        await_bytes(arx.at[a, pl.ds(0, PX - 1)], ar_send.at[a, 0])
        await_bytes(ary.at[a, pl.ds(0, PY - 1)], ar_send.at[a, 1])
    store_d.wait()
    store_x.wait()
    store_r.wait()


def scratch(PX, PY, XL, N):
    NZ = PX
    field = pltpu.VMEM((NZ, ROWS, XL), F32)
    padded = pltpu.VMEM((NZ, ROWS + 16, XL), F32)
    blocks = pltpu.VMEM((2, PX, ROWS, XL), BF16)
    tiles = pltpu.VMEM((2, PY, 32, 128), BF16)
    dma = pltpu.SemaphoreType.DMA
    return [
        pltpu.VMEM((N, N), BF16),
        pltpu.VMEM((NZ, ROWS, XL), jnp.int32),
        field,
        field,
        field,
        padded,
        padded,
        padded,
        padded,
        field,
        field,
        field,
        field,
        field,
        field,
        pltpu.VMEM((NZ + 1, ROWS, XL), F32),
        field,
        field,
        blocks,
        blocks,
        tiles,
        tiles,
        tiles,
        tiles,
        blocks,
        blocks,
        pltpu.VMEM((ROWS, N), BF16),
        pltpu.VMEM((ROWS, N), F32),
        pltpu.VMEM((ROWS, N), BF16),
        pltpu.VMEM((ROWS, N), F32),
        pltpu.VMEM((128, 128), F32),
        pltpu.VMEM((3, 2, 2 * NZ, XL), F32),
        pltpu.VMEM((3, 2, 2 * NZ, XL), F32),
        pltpu.VMEM((3, 16, NZ * ROWS), F32),
        pltpu.VMEM((3, 2, 16, NZ * ROWS), F32),
        pltpu.VMEM((3, 1, 1, 256), F32),
        pltpu.VMEM((3, PX, 1, 256), F32),
        pltpu.VMEM((3, 1, 1, 256), F32),
        pltpu.VMEM((3, PY, 1, 256), F32),
        dma((4,)),
        dma((3,)),
        dma((3, 4)),
        dma((3, 4)),
        dma((2, 4)),
        dma((2, 4)),
        dma((3, 2)),
        dma((3, 2)),
    ]


def shards(PX, PY, right_side, solution_in, classes, coeff_table, eigenvectors, eigenvalues, level_shift):
    XL, N = right_side.shape[2], eigenvectors.shape[0]
    out = jax.ShapeDtypeStruct(right_side.shape, F32)
    hbm = pl.BlockSpec(memory_space=pl.ANY)
    smem = pl.BlockSpec(memory_space=pltpu.SMEM)
    vmem = pl.BlockSpec(memory_space=pltpu.VMEM)
    return tuple(
        pl.pallas_call(
            functools.partial(kernel, PX, PY),
            out_shape=[out, out, out],
            in_specs=[hbm, hbm, hbm, smem, hbm, vmem, smem],
            out_specs=[hbm, hbm, hbm],
            scratch_shapes=scratch(PX, PY, XL, N),
            compiler_params=pltpu.CompilerParams(
                collective_id=0, has_side_effects=True, vmem_limit_bytes=50 * 2**20
            ),
        )(
            right_side,
            solution_in,
            classes,
            coeff_table,
            eigenvectors,
            eigenvalues.reshape(1, N),
            level_shift,
        )
    )


def solution(mesh):
    field = P(None, "py", "px")
    return jax.shard_map(
        functools.partial(shards, mesh.shape["px"], mesh.shape["py"]),
        mesh=mesh,
        in_specs=(field, field, field, P(), P(), P(), P()),
        out_specs=(field, field, field),
        check_vma=False,
    )
```

```python
import functools

import jax
import jax.numpy as jnp
from jax import lax
from jax.experimental import pallas as pl
from jax.experimental.pallas import tpu as pltpu
from jax.sharding import PartitionSpec as P

F32 = jnp.float32
BF16 = jnp.bfloat16
ROWS = 64
TOP, END = 8, 8 + ROWS
HIGH = lax.Precision.HIGHEST
NT = (((1,), (1,)), ((), ()))
TN = (((0,), (0,)), ((), ()))


def scratch(PX, PY, XL, N):
    NZ = PX
    field = pltpu.VMEM((NZ, ROWS, XL), F32)
    padded = pltpu.VMEM((NZ, ROWS + 16, XL), F32)
    lines = pltpu.VMEM((ROWS, N), F32)
    padded_lines = pltpu.VMEM((ROWS + 16, N), F32)
    tiles = pltpu.VMEM((2, PY, 32, 128), BF16)
    dma = pltpu.SemaphoreType.DMA
    return dict(
        vec=pltpu.VMEM((N, N), BF16),
        eig=pltpu.VMEM((1, N), F32),
        table=pltpu.SMEM((16,), F32),
        shift=pltpu.SMEM((NZ,), F32),
        cls=pltpu.VMEM((NZ, ROWS, XL), jnp.int32),
        sol=field,
        res=field,
        direction=field,
        image=field,
        vp_x=padded,
        vp_0=padded,
        vp_1=padded,
        cp=padded,
        halo=field,
        chalo=field,
        w_e=field,
        w_w=field,
        w_s=field,
        w_n=field,
        w_z=pltpu.VMEM((NZ + 1, ROWS, XL), F32),
        w_sum=field,
        cls_send=pltpu.VMEM((NZ + 2, ROWS, XL), BF16),
        cls_recv=pltpu.VMEM((PX, 3, ROWS, XL), BF16),
        pc=padded_lines,
        p_e=lines,
        p_w=lines,
        p_s=lines,
        p_n=lines,
        p_u=lines,
        p_d=lines,
        p_sum=lines,
        zp=pltpu.VMEM((2, ROWS + 16, N), F32),
        above=pltpu.VMEM((2, PX, ROWS, XL), BF16),
        below=pltpu.VMEM((2, PX, ROWS, XL), BF16),
        row_send=pltpu.VMEM((3, 2, 1, N), F32),
        row_recv=pltpu.VMEM((3, 2, 1, N), F32),
        xsend=pltpu.VMEM((PX, ROWS, XL), BF16),
        xrecv=pltpu.VMEM((PX, ROWS, XL), BF16),
        ysend=tiles,
        yrecv=tiles,
        zsend=tiles,
        zrecv=tiles,
        bsend=pltpu.VMEM((2, PX, ROWS, XL), BF16),
        brecv=pltpu.VMEM((2, PX, ROWS, XL), BF16),
        lhs=pltpu.VMEM((ROWS, N), BF16),
        s2=lines,
        s3=pltpu.VMEM((ROWS, N), BF16),
        dinv=lines,
        eigc=pltpu.VMEM((128, 128), F32),
        rsend=pltpu.VMEM((3, 2, 2 * NZ, XL), F32),
        rrecv=pltpu.VMEM((3, 2, 2 * NZ, XL), F32),
        csend=pltpu.VMEM((3, 8, NZ * ROWS), F32),
        crecv=pltpu.VMEM((3, 16, NZ * ROWS), F32),
        arx_send=pltpu.VMEM((3, 1, 1, 256), F32),
        arx=pltpu.VMEM((3, PX, 1, 256), F32),
        ary_send=pltpu.VMEM((3, 1, 1, 256), F32),
        ary=pltpu.VMEM((3, PY, 1, 256), F32),
        load_sem=dma((7,)),
        store_sem=dma((3,)),
        halo_send=dma((3, 4)),
        halo_recv=dma((3, 4)),
        cls_sem=dma((2,)),
        line_send=dma((3, 4)),
        line_recv=dma((3, 4)),
        a2a_send=dma((2, 4)),
        a2a_recv=dma((2, 4)),
        ar_send=dma((3, 2)),
        ar_recv=dma((3, 2)),
    )


def kernel(PX, PY, names, *refs):
    b_hbm, x_hbm, cls_hbm, table_hbm, vec_hbm, eig_hbm, shift_hbm, sol_hbm, res_hbm, dir_hbm = refs[:10]
    R = dict(zip(names, refs[10:]))
    vec, eig, table, shift, cls = (R[n] for n in ("vec", "eig", "table", "shift", "cls"))
    sol, res, direction, image = (R[n] for n in ("sol", "res", "direction", "image"))
    vp_x, vp_0, vp_1, cp, halo, chalo = (R[n] for n in ("vp_x", "vp_0", "vp_1", "cp", "halo", "chalo"))
    w_e, w_w, w_s, w_n, w_z, w_sum = (R[n] for n in ("w_e", "w_w", "w_s", "w_n", "w_z", "w_sum"))
    p_e, p_w, p_s, p_n, p_u, p_d, p_sum = (
        R[n] for n in ("p_e", "p_w", "p_s", "p_n", "p_u", "p_d", "p_sum")
    )
    cls_send, cls_recv, pc, zp = (R[n] for n in ("cls_send", "cls_recv", "pc", "zp"))
    above, below, row_send, row_recv = (R[n] for n in ("above", "below", "row_send", "row_recv"))
    xsend, xrecv, ysend, yrecv = (R[n] for n in ("xsend", "xrecv", "ysend", "yrecv"))
    zsend, zrecv, bsend, brecv = (R[n] for n in ("zsend", "zrecv", "bsend", "brecv"))
    lhs, s2, s3, dinv, eigc = (R[n] for n in ("lhs", "s2", "s3", "dinv", "eigc"))
    rsend, rrecv, csend, crecv = (R[n] for n in ("rsend", "rrecv", "csend", "crecv"))
    arx_send, arx, ary_send, ary = (R[n] for n in ("arx_send", "arx", "ary_send", "ary"))
    load_sem, store_sem, halo_send, halo_recv = (
        R[n] for n in ("load_sem", "store_sem", "halo_send", "halo_recv")
    )
    cls_sem, line_send, line_recv = (R[n] for n in ("cls_sem", "line_send", "line_recv"))
    a2a_send, a2a_recv, ar_send, ar_recv = (
        R[n] for n in ("a2a_send", "a2a_recv", "ar_send", "ar_recv")
    )

    NZ, XL, N = PX, image.shape[2], vec.shape[0]
    G = N // 256
    p, q = lax.axis_index("px"), lax.axis_index("py")
    pending = []
    far = sorted(range(1, PX), key=lambda t: -min(t, PX - t))

    def lane(shape):
        return lax.broadcasted_iota(jnp.int32, shape, len(shape) - 1)

    def row(shape):
        return lax.broadcasted_iota(jnp.int32, shape, len(shape) - 2)

    def block(i, size):
        return pl.ds(pl.multiple_of(i * size, size), size)

    def remote(src, dst, send, recv, where):
        return pltpu.make_async_remote_copy(
            src_ref=src, dst_ref=dst, send_sem=send, recv_sem=recv, device_id=where
        )

    def await_bytes(ref, sem):
        pltpu.make_async_copy(ref, ref, sem).wait()

    def sent_later(ref, sem):
        pending.append(lambda: await_bytes(ref, sem))

    north = {"py": lax.rem(q + PY - 1, PY)}
    south = {"py": lax.rem(q + 1, PY)}
    west_of = {"px": lax.rem(p + PX - 1, PX)}
    east_of = {"px": lax.rem(p + 1, PX)}
    has_north = jnp.where(q > 0, 1.0, 0.0).astype(F32)
    has_south = jnp.where(q < PY - 1, 1.0, 0.0).astype(F32)
    has_first = jnp.where(p > 0, 1.0, 0.0).astype(F32)
    has_last = jnp.where(p < PX - 1, 1.0, 0.0).astype(F32)

    load_cls = pltpu.make_async_copy(cls_hbm, cls, load_sem.at[0])
    load_x = pltpu.make_async_copy(x_hbm, vp_x.at[:, TOP:END, :], load_sem.at[1])
    load_b = pltpu.make_async_copy(b_hbm, res, load_sem.at[2])
    load_v = pltpu.make_async_copy(vec_hbm, vec, load_sem.at[3])
    load_t = pltpu.make_async_copy(table_hbm, table, load_sem.at[4])
    load_s = pltpu.make_async_copy(shift_hbm, shift, load_sem.at[5])
    load_e = pltpu.make_async_copy(eig_hbm, eig, load_sem.at[6])
    for load in (load_x, load_cls, load_t, load_s, load_e, load_b, load_v):
        load.start()

    barrier = pltpu.get_barrier_semaphore()

    @pl.loop(1, PX)
    def _(t):
        pl.semaphore_signal(barrier, inc=1, device_id={"px": lax.rem(p + t, PX)})

    @pl.loop(1, PY)
    def _(t):
        pl.semaphore_signal(barrier, inc=1, device_id={"py": lax.rem(q + t, PY)})

    def pick(base, kind, rows):
        r, l = row((rows, XL)), lane((rows, XL))
        hot = ((r == base) & (l == 0)) | ((r == base + 1) & (l == XL - 1))
        return jnp.where(hot, 1.0, 0.0).astype(kind)

    def place(base):
        r, l = row((16, XL)), lane((16, XL))
        hot_l = jnp.where((r == base + 1) & (l == 0), has_first, 0.0)
        hot_r = jnp.where((r == 8 + base) & (l == XL - 1), has_last, 0.0)
        return hot_l + hot_r

    def lookup(values):
        result = jnp.zeros(values.shape, F32)
        for label in range(16):
            result = jnp.where(values == label, table[label], result)
        return result

    def halo_copies(h):
        return [
            remote(rsend.at[h, 0], rrecv.at[h, 1], halo_send.at[h, 0], halo_recv.at[h, 0], north),
            remote(rsend.at[h, 1], rrecv.at[h, 0], halo_send.at[h, 1], halo_recv.at[h, 1], south),
            remote(csend.at[h], crecv.at[h, pl.ds(8, 8)], halo_send.at[h, 2], halo_recv.at[h, 2], west_of),
            remote(csend.at[h], crecv.at[h, pl.ds(0, 8)], halo_send.at[h, 3], halo_recv.at[h, 3], east_of),
        ]

    def start(copies):
        for copy in copies:
            copy.start()
            pending.append(copy.wait_send)
        return copies

    load_x.wait()
    load_cls.wait()
    for k in range(NZ):
        rsend[0, 0, k : k + 1, :] = vp_x[k, TOP : TOP + 1, :]
        rsend[0, 1, k : k + 1, :] = vp_x[k, END - 1 : END, :]
        rsend[0, 0, NZ + k : NZ + k + 1, :] = cls[k, 0:1, :].astype(F32)
        rsend[0, 1, NZ + k : NZ + k + 1, :] = cls[k, ROWS - 1 : ROWS, :].astype(F32)
    x_flat = vp_x[:, TOP:END, :].reshape(NZ * ROWS, XL)
    cls_flat = cls[...].reshape(NZ * ROWS, XL).astype(F32).astype(BF16)
    csend[0] = lax.dot_general(
        pick(0, F32, 8), x_flat, NT, precision=HIGH, preferred_element_type=F32
    ) + lax.dot_general(pick(2, BF16, 16), cls_flat, NT, preferred_element_type=F32)[0:8]
    cls_send[1 : NZ + 1] = cls_flat.reshape(NZ, ROWS, XL)
    cls_send[0] = jnp.zeros((ROWS, XL), BF16)
    cls_send[NZ + 1] = jnp.zeros((ROWS, XL), BF16)
    load_t.wait()
    load_s.wait()
    load_e.wait()
    pl.semaphore_wait(barrier, PX - 1 + PY - 1)
    copies = start(halo_copies(0))

    @pl.loop(0, NZ)
    def _(k):
        cp[k, TOP:END, :] = lookup(cls[k])

    w_z[0] = jnp.zeros((ROWS, XL), F32)
    w_z[NZ] = jnp.zeros((ROWS, XL), F32)

    @pl.loop(0, NZ - 1)
    def _(k):
        w_z[k + 1] = 0.5 * (cp[k, TOP:END, :] + cp[k + 1, TOP:END, :])

    group, part = q // 4, lax.rem(q, 4)
    for half in range(2):
        cols = pl.ds(pl.multiple_of(group * 256 + half * 128, 128), 128)
        eigc[...] = jnp.broadcast_to(eig[:, cols], (128, 128)).T
        mine = eigc[block(part, 32), 0:1] + shift[p]
        dinv[half * 32 : half * 32 + 32, :] = 1.0 / (mine + eig[...])

    def wait_all(copies):
        for copy in copies:
            copy.wait_recv()

    def fill_rows(h, vp):
        for k in range(NZ):
            vp[k, TOP - 1 : TOP, :] = rrecv[h, 0, k : k + 1, :] * has_north
            vp[k, END : END + 1, :] = rrecv[h, 1, k : k + 1, :] * has_south

    wait_all(copies)
    fill_rows(0, vp_x)
    for k in range(NZ):
        cp[k, TOP - 1 : TOP, :] = lookup(rrecv[0, 0, NZ + k : NZ + k + 1, :]) * has_north
        cp[k, END : END + 1, :] = lookup(rrecv[0, 1, NZ + k : NZ + k + 1, :]) * has_south

    def columns(values, base, precision, kind):
        out = lax.dot_general(
            values.astype(kind),
            place(base).astype(kind),
            TN,
            precision=precision,
            preferred_element_type=F32,
        )
        return out.reshape(NZ, ROWS, XL)

    halo[...] = columns(crecv[0], 0, HIGH, F32)
    chalo[...] = columns(lookup(crecv[0]), 2, HIGH, F32)

    lanes = lane((ROWS, XL))

    def east(values, edge):
        return jnp.where(lanes == XL - 1, edge, pltpu.roll(values, XL - 1, 1))

    def west(values, edge):
        return jnp.where(lanes == 0, edge, pltpu.roll(values, 1, 1))

    @pl.loop(0, NZ)
    def _(k):
        here = cp[k, TOP:END, :]
        edge = chalo[k]
        to_e = 0.5 * (here + east(here, edge))
        to_w = 0.5 * (here + west(here, edge))
        to_n = 0.5 * (here + cp[k, TOP - 1 : END - 1, :])
        to_s = 0.5 * (here + cp[k, TOP + 1 : END + 1, :])
        w_e[k] = to_e
        w_w[k] = to_w
        w_n[k] = to_n
        w_s[k] = to_s
        w_sum[k] = to_e + to_w + to_n + to_s + w_z[k] + w_z[k + 1]

    def operator(vp, k):
        here = vp[k, TOP:END, :]
        edge = halo[k]
        lower = vp[jnp.maximum(k - 1, 0), TOP:END, :]
        upper = vp[jnp.minimum(k + 1, NZ - 1), TOP:END, :]
        out = w_sum[k] * here - w_e[k] * east(here, edge) - w_w[k] * west(here, edge)
        out = out - w_n[k] * vp[k, TOP - 1 : END - 1, :] - w_s[k] * vp[k, TOP + 1 : END + 1, :]
        return out - w_z[k] * lower - w_z[k + 1] * upper

    def fold(values):
        part = values.reshape(values.shape[0] // 8, 8, values.shape[1]).sum(0)
        out = part[:, :128]
        for c in range(128, values.shape[1], 128):
            out = out + part[:, c : c + 128]
        return out

    load_b.wait()
    for t in far + [0]:
        k = lax.rem(p + t, NZ)
        value = res[k] - operator(vp_x, k)
        res[k] = value
        if t:
            xsend[k] = value.astype(BF16)
            remote(
                xsend.at[k], xrecv.at[p], a2a_send.at[0, 0], a2a_recv.at[0, 0], {"px": k}
            ).start()
        else:
            xrecv[p] = value.astype(BF16)
    sent_later(xsend.at[pl.ds(0, PX - 1)], a2a_send.at[0, 0])

    for t in far:
        dest = lax.rem(p + t, PX)
        remote(
            cls_send.at[pl.ds(dest, 3)], cls_recv.at[p], cls_sem.at[0], cls_sem.at[1], {"px": dest}
        ).start()
    cls_recv[p] = cls_send[pl.ds(p, 3)]
    sent_later(cls_recv.at[pl.ds(0, PX - 1)], cls_sem.at[0])

    load_v.wait()

    half_lane = lane((32, 128)) < 64

    def product(ref, cols):
        return jnp.dot(ref[...], vec[:, cols], preferred_element_type=F32)

    def scatter_tile(src, dst, it, which, t, g):
        for u in range(4):
            if t == 0 and u == 0:
                dst[it, q] = src[it, q]
                continue
            dest = g * 4 + (lax.rem(q + u, 4) if t == 0 else u)
            remote(
                src.at[it, dest], dst.at[it, q], a2a_send.at[it, which], a2a_recv.at[it, which], {"py": dest}
            ).start()

    def x_forward(it):
        for t in list(range(1, G)) + [0]:
            g = lax.rem(q // 4 + t, G)
            tile = product(lhs, block(g, 256))
            turned = jnp.concatenate([tile[:, :128], tile[:, 128:]], axis=0).T
            ysend[it, block(g, 4)] = turned.astype(BF16).reshape(4, 32, 128)
            scatter_tile(ysend, yrecv, it, 1, t, g)
        sent_later(ysend.at[it, pl.ds(0, PY - 1)], a2a_send.at[it, 1])

    def y_arrive(it):
        await_bytes(yrecv.at[it, pl.ds(0, PY - 1)], a2a_recv.at[it, 1])
        for m in range(PY // 2):
            even, odd = yrecv[it, 2 * m].astype(F32), yrecv[it, 2 * m + 1].astype(F32)
            low = jnp.where(half_lane, even, pltpu.roll(odd, 64, 1))
            high = jnp.where(half_lane, pltpu.roll(even, 64, 1), odd)
            lhs[0:32, m * 128 : (m + 1) * 128] = low.astype(BF16)
            lhs[32:64, m * 128 : (m + 1) * 128] = high.astype(BF16)

    def spectral(it, alpha):
        acc = jnp.zeros((8, 128), F32)
        for t in range(G):
            cols = slice(t * 256, (t + 1) * 256)
            tile = product(lhs, cols)
            if it == 0:
                s2[:, cols] = tile
            else:
                tile = s2[:, cols] - alpha * tile
            scaled = (tile * dinv[:, cols]).astype(BF16)
            s3[:, cols] = scaled
            acc = acc + fold(tile * scaled.astype(F32))
        return acc

    def y_back(it):
        for t in list(range(1, G)) + [0]:
            g = lax.rem(q // 4 + t, G)
            tile = product(s3, block(g, 256))
            for h in range(2):
                low, high = tile[0:32, h * 128 : h * 128 + 128], tile[32:64, h * 128 : h * 128 + 128]
                even = jnp.where(half_lane, low, pltpu.roll(high, 64, 1))
                odd = jnp.where(half_lane, pltpu.roll(low, 64, 1), high)
                zsend[it, g * 4 + 2 * h] = even.astype(BF16)
                zsend[it, g * 4 + 2 * h + 1] = odd.astype(BF16)
            scatter_tile(zsend, zrecv, it, 2, t, g)
        sent_later(zsend.at[it, pl.ds(0, PY - 1)], a2a_send.at[it, 2])

    def z_arrive(it):
        await_bytes(zrecv.at[it, pl.ds(0, PY - 1)], a2a_recv.at[it, 2])
        for g in range(G):
            turned = zrecv[it, 4 * g : 4 * g + 4].reshape(128, 128).astype(F32).T.astype(BF16)
            lhs[:, g * 256 : g * 256 + 128] = turned[0:64]
            lhs[:, g * 256 + 128 : g * 256 + 256] = turned[64:128]

    def line_copies(h):
        return [
            remote(row_send.at[h, 0], row_recv.at[h, 1], line_send.at[h, 0], line_recv.at[h, 0], north),
            remote(row_send.at[h, 1], row_recv.at[h, 0], line_send.at[h, 1], line_recv.at[h, 1], south),
        ]

    def x_back(it):
        for c in range(PX):
            tile = product(lhs, slice(c * XL, (c + 1) * XL)).astype(BF16)
            bsend[it, c] = tile
            zp[it, TOP:END, c * XL : (c + 1) * XL] = tile.astype(F32)
            remote(
                bsend.at[it, c], above.at[it, c], line_send.at[it, 2], line_recv.at[it, 2], west_of
            ).start()
            remote(
                bsend.at[it, c], below.at[it, c], line_send.at[it, 3], line_recv.at[it, 3], east_of
            ).start()
        row_send[it, 0] = zp[it, TOP : TOP + 1, :]
        row_send[it, 1] = zp[it, END - 1 : END, :]
        rows = start(line_copies(it))
        sent_later(bsend.at[it], line_send.at[it, 2])
        sent_later(bsend.at[it], line_send.at[it, 3])
        for t in far:
            c = lax.rem(p + t, PX)
            remote(
                bsend.at[it, c], brecv.at[it, p], a2a_send.at[it, 3], a2a_recv.at[it, 3], {"px": c}
            ).start()
        brecv[it, p] = bsend[it, p]
        sent_later(bsend.at[it, pl.ds(0, PX - 1)], a2a_send.at[it, 3])
        return rows

    def plane(which):
        return jnp.concatenate([cls_recv[c, which] for c in range(PX)], axis=1).astype(F32)

    def pencil_coefficients():
        await_bytes(cls_recv.at[pl.ds(0, PX - 1)], cls_sem.at[1])
        for c in range(PX):
            pc[TOP:END, c * XL : (c + 1) * XL] = lookup(cls_recv[c, 1].astype(F32))
        row_send[2, 0] = pc[TOP : TOP + 1, :]
        row_send[2, 1] = pc[END - 1 : END, :]
        rows = start(line_copies(2))
        for c in range(PX):
            cols = slice(c * XL, (c + 1) * XL)
            here = pc[TOP:END, cols]
            p_d[:, cols] = 0.5 * has_first * (here + lookup(cls_recv[c, 0].astype(F32)))
            p_u[:, cols] = 0.5 * has_last * (here + lookup(cls_recv[c, 2].astype(F32)))
        return rows

    wide = lane((16, N))

    def pencil_weights(rows):
        wait_all(rows)
        pc[TOP - 1 : TOP, :] = row_recv[2, 0] * has_north
        pc[END : END + 1, :] = row_recv[2, 1] * has_south
        for r in range(0, ROWS, 16):
            at = slice(r, r + 16)
            here = pc[TOP + r : TOP + r + 16, :]
            to_e = 0.5 * (here + jnp.where(wide == N - 1, 0.0, pltpu.roll(here, N - 1, 1)))
            to_w = 0.5 * (here + jnp.where(wide == 0, 0.0, pltpu.roll(here, 1, 1)))
            to_n = 0.5 * (here + pc[TOP - 1 + r : TOP + 15 + r, :])
            to_s = 0.5 * (here + pc[TOP + 1 + r : TOP + 17 + r, :])
            p_e[at, :] = jnp.where(wide == N - 1, 0.0, to_e)
            p_w[at, :] = jnp.where(wide == 0, 0.0, to_w)
            p_n[at, :] = to_n
            p_s[at, :] = to_s
            p_sum[at, :] = to_e + to_w + to_n + to_s + p_u[at, :] + p_d[at, :]

    def beside(ref, it, r):
        return jnp.concatenate([ref[it, c, r : r + 16, :] for c in range(PX)], axis=1).astype(F32)

    def pencil_operator(it, rows, beta):
        wait_all(rows)
        zp[it, TOP - 1 : TOP, :] = row_recv[it, 0] * has_north
        zp[it, END : END + 1, :] = row_recv[it, 1] * has_south
        if it == 1:
            for r in range(0, ROWS + 16, 16):
                if r == 0:
                    at = slice(TOP - 1, 16)
                elif r == ROWS:
                    at = slice(ROWS, END + 1)
                else:
                    at = slice(r, r + 16)
                zp[1, at, :] = zp[1, at, :] + beta * zp[0, at, :]
        await_bytes(above.at[it], line_recv.at[it, 2])
        await_bytes(below.at[it], line_recv.at[it, 3])
        acc = jnp.zeros((8, 128), F32)
        for r in range(0, ROWS, 16):
            at = slice(r, r + 16)
            here = zp[it, TOP + r : TOP + r + 16, :]
            up, down = beside(above, it, r), beside(below, it, r)
            if it == 1:
                up = up + beta * beside(above, 0, r)
                down = down + beta * beside(below, 0, r)
            out = p_sum[at, :] * here - p_e[at, :] * pltpu.roll(here, N - 1, 1)
            out = out - p_w[at, :] * pltpu.roll(here, 1, 1)
            out = out - p_n[at, :] * zp[it, TOP - 1 + r : TOP + 15 + r, :]
            out = out - p_s[at, :] * zp[it, TOP + 1 + r : TOP + 17 + r, :]
            out = out - p_u[at, :] * up - p_d[at, :] * down
            if it == 0:
                lhs[at, :] = out.astype(BF16)
            acc = acc + fold(here * out)
        return acc

    def reduce_start(a, first, second_part):
        mine = jnp.concatenate(
            [first.sum(0, keepdims=True), second_part.sum(0, keepdims=True)], axis=1
        )
        arx_send[a, 0] = mine
        arx[a, p] = mine
        for t in far:
            dest = lax.rem(p + t, PX)
            remote(
                arx_send.at[a, 0], arx.at[a, p], ar_send.at[a, 0], ar_recv.at[a, 0], {"px": dest}
            ).start()
        sent_later(arx.at[a, pl.ds(0, PX - 1)], ar_send.at[a, 0])

    def reduce_middle(a):
        await_bytes(arx.at[a, pl.ds(0, PX - 1)], ar_recv.at[a, 0])
        mine = arx[a, 0]
        for t in range(1, PX):
            mine = mine + arx[a, t]
        ary_send[a, 0] = mine
        ary[a, q] = mine

        @pl.loop(1, PY)
        def _(t):
            dest = lax.rem(q + t, PY)
            remote(
                ary_send.at[a, 0], ary.at[a, q], ar_send.at[a, 1], ar_recv.at[a, 1], {"py": dest}
            ).start()

        sent_later(ary.at[a, pl.ds(0, PY - 1)], ar_send.at[a, 1])

    def reduce_end(a):
        await_bytes(ary.at[a, pl.ds(0, PY - 1)], ar_recv.at[a, 1])
        total = ary[a, 0]
        for t in range(1, PY):
            total = total + ary[a, t]
        return (
            total[:, :128].sum(1, keepdims=True),
            total[:, 128:].sum(1, keepdims=True),
        )

    zero = jnp.zeros((8, 128), F32)

    def direction_halo(h, vp):
        for k in range(NZ):
            rsend[h, 0, k : k + 1, :] = vp[k, TOP : TOP + 1, :]
            rsend[h, 1, k : k + 1, :] = vp[k, END - 1 : END, :]
            rsend[h, :, NZ + k : NZ + k + 1, :] = jnp.zeros((2, 1, XL), F32)
        flat = vp[:, TOP:END, :].reshape(NZ * ROWS, XL).astype(BF16)
        csend[h] = lax.dot_general(pick(0, BF16, 16), flat, NT, preferred_element_type=F32)[0:8]
        return start(halo_copies(h))

    def direction_edges(h, vp, copies):
        wait_all(copies)
        fill_rows(h, vp)
        halo[...] = columns(crecv[h], 0, None, BF16)

    await_bytes(xrecv.at[pl.ds(0, PX - 1)], a2a_recv.at[0, 0])
    for c in range(PX):
        lhs[:, c * XL : (c + 1) * XL] = xrecv[c]
    x_forward(0)
    y_arrive(0)
    gamma_part = spectral(0, None)
    y_back(0)
    coeff_rows = pencil_coefficients()
    z_arrive(0)
    rows = x_back(0)
    pencil_weights(coeff_rows)
    curve = pencil_operator(0, rows, None)
    reduce_start(0, gamma_part, curve)

    x_forward(1)
    reduce_middle(0)
    await_bytes(brecv.at[0, pl.ds(0, PX - 1)], a2a_recv.at[0, 3])

    @pl.loop(0, NZ)
    def _(k):
        vp_0[k, TOP:END, :] = brecv[0, k].astype(F32)

    copies = direction_halo(1, vp_0)
    y_arrive(1)
    gamma0, curve0 = reduce_end(0)
    alpha0 = gamma0 / curve0
    reduce_start(1, spectral(1, alpha0), zero)
    y_back(1)
    direction_edges(1, vp_0, copies)

    @pl.loop(0, NZ)
    def _(k):
        res[k] = res[k] - alpha0 * operator(vp_0, k)
        sol[k] = vp_x[k, TOP:END, :] + alpha0 * vp_0[k, TOP:END, :]

    reduce_middle(1)
    z_arrive(1)
    rows = x_back(1)
    gamma1, _ = reduce_end(1)
    beta = gamma1 / gamma0
    reduce_start(2, pencil_operator(1, rows, beta), zero)

    await_bytes(brecv.at[1, pl.ds(0, PX - 1)], a2a_recv.at[1, 3])

    @pl.loop(0, NZ)
    def _(k):
        value = brecv[1, k].astype(F32) + beta * vp_0[k, TOP:END, :]
        vp_1[k, TOP:END, :] = value
        direction[k] = value

    copies = direction_halo(2, vp_1)
    store_d = pltpu.make_async_copy(direction, dir_hbm, store_sem.at[0])
    store_d.start()
    reduce_middle(2)
    direction_edges(2, vp_1, copies)

    @pl.loop(0, NZ)
    def _(k):
        image[k] = operator(vp_1, k)

    curve1, _ = reduce_end(2)
    alpha1 = gamma1 / curve1

    @pl.loop(0, NZ)
    def _(k):
        sol[k] = sol[k] + alpha1 * direction[k]
        res[k] = res[k] - alpha1 * image[k]

    store_x = pltpu.make_async_copy(sol, sol_hbm, store_sem.at[1])
    store_r = pltpu.make_async_copy(res, res_hbm, store_sem.at[2])
    store_x.start()
    store_r.start()

    for wait in pending:
        wait()
    store_d.wait()
    store_x.wait()
    store_r.wait()


def shards(PX, PY, right_side, solution_in, classes, coeff_table, eigenvectors, eigenvalues, level_shift):
    XL, N = right_side.shape[2], eigenvectors.shape[0]
    out = jax.ShapeDtypeStruct(right_side.shape, F32)
    hbm = pl.BlockSpec(memory_space=pl.ANY)
    buffers = scratch(PX, PY, XL, N)
    return tuple(
        pl.pallas_call(
            functools.partial(kernel, PX, PY, tuple(buffers)),
            out_shape=[out, out, out],
            in_specs=[hbm] * 7,
            out_specs=[hbm, hbm, hbm],
            scratch_shapes=list(buffers.values()),
            compiler_params=pltpu.CompilerParams(
                collective_id=0, has_side_effects=True, vmem_limit_bytes=60 * 2**20
            ),
        )(
            right_side,
            solution_in,
            classes,
            coeff_table,
            eigenvectors,
            eigenvalues.reshape(1, N),
            level_shift,
        )
    )


def solution(mesh):
    field = P(None, "py", "px")
    return jax.shard_map(
        functools.partial(shards, mesh.shape["px"], mesh.shape["py"]),
        mesh=mesh,
        in_specs=(field, field, field, P(), P(), P(), P()),
        out_specs=(field, field, field),
        check_vma=False,
    )
```

```python
import functools

import jax
import jax.numpy as jnp
from jax import lax
from jax.experimental import pallas as pl
from jax.experimental.pallas import tpu as pltpu
from jax.sharding import PartitionSpec as P

F32 = jnp.float32
BF16 = jnp.bfloat16
ROWS = 64
TOP, END = 8, 8 + ROWS
HIGH = lax.Precision.HIGHEST
NT = (((1,), (1,)), ((), ()))
TN = (((0,), (0,)), ((), ()))


def scratch(PX, PY, XL, N):
    NZ = PX
    field = pltpu.VMEM((NZ, ROWS, XL), F32)
    padded = pltpu.VMEM((NZ, ROWS + 16, XL), F32)
    lines = pltpu.VMEM((ROWS, N), F32)
    padded_lines = pltpu.VMEM((ROWS + 16, N), F32)
    tiles = pltpu.VMEM((2, PY, 32, 128), BF16)
    dma = pltpu.SemaphoreType.DMA
    return dict(
        vec=pltpu.VMEM((N, N), BF16),
        eig=pltpu.VMEM((1, N), F32),
        table=pltpu.SMEM((16,), F32),
        shift=pltpu.SMEM((NZ,), F32),
        cls=pltpu.VMEM((NZ, ROWS, XL), jnp.int32),
        sol=field,
        res=field,
        direction=field,
        image=field,
        vp_x=padded,
        vp_0=padded,
        vp_1=padded,
        cp=padded,
        halo=field,
        chalo=field,
        w_e=field,
        w_w=field,
        w_s=field,
        w_n=field,
        w_z=pltpu.VMEM((NZ + 1, ROWS, XL), F32),
        w_sum=field,
        cls_send=pltpu.VMEM((NZ, ROWS, XL), BF16),
        cls_recv=pltpu.VMEM((3, PX, ROWS, XL), BF16),
        pc=padded_lines,
        p_e=lines,
        p_w=lines,
        p_s=lines,
        p_n=lines,
        p_u=lines,
        p_d=lines,
        p_sum=lines,
        zp=pltpu.VMEM((2, ROWS + 16, N), F32),
        above=pltpu.VMEM((2, PX, ROWS, XL), BF16),
        below=pltpu.VMEM((2, PX, ROWS, XL), BF16),
        row_send=pltpu.VMEM((3, 2, 1, N), F32),
        row_recv=pltpu.VMEM((3, 2, 1, N), F32),
        xsend=pltpu.VMEM((PX, ROWS, XL), BF16),
        xrecv=pltpu.VMEM((PX, ROWS, XL), BF16),
        ysend=tiles,
        yrecv=tiles,
        zsend=tiles,
        zrecv=tiles,
        bsend=pltpu.VMEM((2, PX, ROWS, XL), BF16),
        brecv=pltpu.VMEM((2, PX, ROWS, XL), BF16),
        lhs=pltpu.VMEM((ROWS, N), BF16),
        s2=lines,
        s3=pltpu.VMEM((ROWS, N), BF16),
        dinv=lines,
        eigc=pltpu.VMEM((128, 128), F32),
        rsend=pltpu.VMEM((1, 2, 2 * NZ, XL), F32),
        rrecv=pltpu.VMEM((1, 2, 2 * NZ, XL), F32),
        csend=pltpu.VMEM((1, 8, NZ * ROWS), F32),
        crecv=pltpu.VMEM((1, 16, NZ * ROWS), F32),
        hrow_send=pltpu.VMEM((2, PX, 2, 1, XL), F32),
        hrow_recv=pltpu.VMEM((2, PX, 2, 1, XL), F32),
        edge_send=pltpu.VMEM((2, PX, 8, ROWS), F32),
        edge_recv=pltpu.VMEM((2, PX, 8, ROWS), F32),
        alpha_out=pltpu.VMEM((1, 128), F32),
        arx_send=pltpu.VMEM((3, 1, 1, 256), F32),
        arx=pltpu.VMEM((3, PX, 1, 256), F32),
        ary_send=pltpu.VMEM((3, 1, 1, 256), F32),
        ary=pltpu.VMEM((3, PY, 1, 256), F32),
        load_sem=dma((7,)),
        store_sem=dma((5,)),
        halo_send=dma((1, 4)),
        halo_recv=dma((1, 4)),
        grid_send=dma((2, 2)),
        grid_recv=dma((2, 2)),
        cls_sem=dma((2, 3)),
        line_send=dma((3, 4)),
        line_recv=dma((3, 4)),
        a2a_send=dma((2, 4)),
        a2a_recv=dma((2, 4)),
        ar_send=dma((3, 2)),
        ar_recv=dma((3, 2)),
    )


def kernel(PX, PY, names, *refs):
    b_hbm, x_hbm, cls_hbm, table_hbm, vec_hbm, eig_hbm, shift_hbm = refs[:7]
    sol_hbm, res_hbm, dir_hbm, image_hbm, alpha_hbm = refs[7:12]
    R = dict(zip(names, refs[12:]))
    vec, eig, table, shift, cls = (R[n] for n in ("vec", "eig", "table", "shift", "cls"))
    sol, res, direction, image = (R[n] for n in ("sol", "res", "direction", "image"))
    vp_x, vp_0, vp_1, cp, halo, chalo = (R[n] for n in ("vp_x", "vp_0", "vp_1", "cp", "halo", "chalo"))
    w_e, w_w, w_s, w_n, w_z, w_sum = (R[n] for n in ("w_e", "w_w", "w_s", "w_n", "w_z", "w_sum"))
    p_e, p_w, p_s, p_n, p_u, p_d, p_sum = (
        R[n] for n in ("p_e", "p_w", "p_s", "p_n", "p_u", "p_d", "p_sum")
    )
    cls_send, cls_recv, pc, zp = (R[n] for n in ("cls_send", "cls_recv", "pc", "zp"))
    above, below, row_send, row_recv = (R[n] for n in ("above", "below", "row_send", "row_recv"))
    xsend, xrecv, ysend, yrecv = (R[n] for n in ("xsend", "xrecv", "ysend", "yrecv"))
    zsend, zrecv, bsend, brecv = (R[n] for n in ("zsend", "zrecv", "bsend", "brecv"))
    lhs, s2, s3, dinv, eigc = (R[n] for n in ("lhs", "s2", "s3", "dinv", "eigc"))
    rsend, rrecv, csend, crecv = (R[n] for n in ("rsend", "rrecv", "csend", "crecv"))
    hrow_send, hrow_recv, edge_send, edge_recv, grid_send, grid_recv, alpha_out = (
        R[n]
        for n in (
            "hrow_send",
            "hrow_recv",
            "edge_send",
            "edge_recv",
            "grid_send",
            "grid_recv",
            "alpha_out",
        )
    )
    arx_send, arx, ary_send, ary = (R[n] for n in ("arx_send", "arx", "ary_send", "ary"))
    load_sem, store_sem, halo_send, halo_recv = (
        R[n] for n in ("load_sem", "store_sem", "halo_send", "halo_recv")
    )
    cls_sem, line_send, line_recv = (R[n] for n in ("cls_sem", "line_send", "line_recv"))
    a2a_send, a2a_recv, ar_send, ar_recv = (
        R[n] for n in ("a2a_send", "a2a_recv", "ar_send", "ar_recv")
    )

    NZ, XL, N = PX, image.shape[2], vec.shape[0]
    G = N // 256
    p, q = lax.axis_index("px"), lax.axis_index("py")
    pending = []
    far = sorted(range(1, PX), key=lambda t: -min(t, PX - t))

    def lane(shape):
        return lax.broadcasted_iota(jnp.int32, shape, len(shape) - 1)

    def row(shape):
        return lax.broadcasted_iota(jnp.int32, shape, len(shape) - 2)

    def block(i, size):
        return pl.ds(pl.multiple_of(i * size, size), size)

    def remote(src, dst, send, recv, where):
        return pltpu.make_async_remote_copy(
            src_ref=src, dst_ref=dst, send_sem=send, recv_sem=recv, device_id=where
        )

    def await_bytes(ref, sem):
        pltpu.make_async_copy(ref, ref, sem).wait()

    def sent_later(ref, sem):
        pending.append(lambda: await_bytes(ref, sem))

    north = {"py": lax.rem(q + PY - 1, PY)}
    south = {"py": lax.rem(q + 1, PY)}
    west_of = {"px": lax.rem(p + PX - 1, PX)}
    east_of = {"px": lax.rem(p + 1, PX)}
    has_north = jnp.where(q > 0, 1.0, 0.0).astype(F32)
    has_south = jnp.where(q < PY - 1, 1.0, 0.0).astype(F32)
    has_first = jnp.where(p > 0, 1.0, 0.0).astype(F32)
    has_last = jnp.where(p < PX - 1, 1.0, 0.0).astype(F32)

    load_cls = pltpu.make_async_copy(cls_hbm, cls, load_sem.at[0])
    load_x = pltpu.make_async_copy(x_hbm, vp_x.at[:, TOP:END, :], load_sem.at[1])
    load_b = pltpu.make_async_copy(b_hbm, res, load_sem.at[2])
    load_v = pltpu.make_async_copy(vec_hbm, vec, load_sem.at[3])
    load_t = pltpu.make_async_copy(table_hbm, table, load_sem.at[4])
    load_s = pltpu.make_async_copy(shift_hbm, shift, load_sem.at[5])
    load_e = pltpu.make_async_copy(eig_hbm, eig, load_sem.at[6])
    for load in (load_x, load_cls, load_t, load_s, load_e, load_b, load_v):
        load.start()

    barrier = pltpu.get_barrier_semaphore()

    @pl.loop(1, PX)
    def _(t):
        pl.semaphore_signal(barrier, inc=1, device_id={"px": lax.rem(p + t, PX)})

    @pl.loop(1, PY)
    def _(t):
        pl.semaphore_signal(barrier, inc=1, device_id={"py": lax.rem(q + t, PY)})

    def pick(base, kind, rows):
        r, l = row((rows, XL)), lane((rows, XL))
        hot = ((r == base) & (l == 0)) | ((r == base + 1) & (l == XL - 1))
        return jnp.where(hot, 1.0, 0.0).astype(kind)

    def place(base):
        r, l = row((16, XL)), lane((16, XL))
        hot_l = jnp.where((r == base + 1) & (l == 0), has_first, 0.0)
        hot_r = jnp.where((r == 8 + base) & (l == XL - 1), has_last, 0.0)
        return hot_l + hot_r

    def lookup(values):
        result = jnp.zeros(values.shape, F32)
        for label in range(16):
            result = jnp.where(values == label, table[label], result)
        return result

    def halo_copies(h):
        return [
            remote(rsend.at[h, 0], rrecv.at[h, 1], halo_send.at[h, 0], halo_recv.at[h, 0], north),
            remote(rsend.at[h, 1], rrecv.at[h, 0], halo_send.at[h, 1], halo_recv.at[h, 1], south),
            remote(csend.at[h], crecv.at[h, pl.ds(8, 8)], halo_send.at[h, 2], halo_recv.at[h, 2], west_of),
            remote(csend.at[h], crecv.at[h, pl.ds(0, 8)], halo_send.at[h, 3], halo_recv.at[h, 3], east_of),
        ]

    def start(copies):
        for copy in copies:
            copy.start()
            pending.append(copy.wait_send)
        return copies

    load_x.wait()
    load_cls.wait()
    for k in range(NZ):
        rsend[0, 0, k : k + 1, :] = vp_x[k, TOP : TOP + 1, :]
        rsend[0, 1, k : k + 1, :] = vp_x[k, END - 1 : END, :]
        rsend[0, 0, NZ + k : NZ + k + 1, :] = cls[k, 0:1, :].astype(F32)
        rsend[0, 1, NZ + k : NZ + k + 1, :] = cls[k, ROWS - 1 : ROWS, :].astype(F32)
    x_flat = vp_x[:, TOP:END, :].reshape(NZ * ROWS, XL)
    cls_flat = cls[...].reshape(NZ * ROWS, XL).astype(F32).astype(BF16)
    csend[0] = lax.dot_general(
        pick(0, F32, 8), x_flat, NT, precision=HIGH, preferred_element_type=F32
    ) + lax.dot_general(pick(2, BF16, 16), cls_flat, NT, preferred_element_type=F32)[0:8]
    cls_send[...] = cls_flat.reshape(NZ, ROWS, XL)
    load_t.wait()
    load_s.wait()
    load_e.wait()
    pl.semaphore_wait(barrier, PX - 1 + PY - 1)
    copies = start(halo_copies(0))

    @pl.loop(0, NZ)
    def _(k):
        cp[k, TOP:END, :] = lookup(cls[k])

    w_z[0] = jnp.zeros((ROWS, XL), F32)
    w_z[NZ] = jnp.zeros((ROWS, XL), F32)

    @pl.loop(0, NZ - 1)
    def _(k):
        w_z[k + 1] = 0.5 * (cp[k, TOP:END, :] + cp[k + 1, TOP:END, :])

    group, part = q // 4, lax.rem(q, 4)
    for half in range(2):
        cols = pl.ds(pl.multiple_of(group * 256 + half * 128, 128), 128)
        eigc[...] = jnp.broadcast_to(eig[:, cols], (128, 128)).T
        mine = eigc[block(part, 32), 0:1] + shift[p]
        dinv[half * 32 : half * 32 + 32, :] = 1.0 / (mine + eig[...])

    def wait_all(copies):
        for copy in copies:
            copy.wait_recv()

    def fill_rows(h, vp):
        for k in range(NZ):
            vp[k, TOP - 1 : TOP, :] = rrecv[h, 0, k : k + 1, :] * has_north
            vp[k, END : END + 1, :] = rrecv[h, 1, k : k + 1, :] * has_south

    wait_all(copies)
    fill_rows(0, vp_x)
    for k in range(NZ):
        cp[k, TOP - 1 : TOP, :] = lookup(rrecv[0, 0, NZ + k : NZ + k + 1, :]) * has_north
        cp[k, END : END + 1, :] = lookup(rrecv[0, 1, NZ + k : NZ + k + 1, :]) * has_south

    def columns(values, base, precision, kind):
        out = lax.dot_general(
            values.astype(kind),
            place(base).astype(kind),
            TN,
            precision=precision,
            preferred_element_type=F32,
        )
        return out.reshape(NZ, ROWS, XL)

    halo[...] = columns(crecv[0], 0, HIGH, F32)
    chalo[...] = columns(lookup(crecv[0]), 2, HIGH, F32)

    lanes = lane((ROWS, XL))

    def east(values, edge):
        return jnp.where(lanes == XL - 1, edge, pltpu.roll(values, XL - 1, 1))

    def west(values, edge):
        return jnp.where(lanes == 0, edge, pltpu.roll(values, 1, 1))

    @pl.loop(0, NZ)
    def _(k):
        here = cp[k, TOP:END, :]
        edge = chalo[k]
        to_e = 0.5 * (here + east(here, edge))
        to_w = 0.5 * (here + west(here, edge))
        to_n = 0.5 * (here + cp[k, TOP - 1 : END - 1, :])
        to_s = 0.5 * (here + cp[k, TOP + 1 : END + 1, :])
        w_e[k] = to_e
        w_w[k] = to_w
        w_n[k] = to_n
        w_s[k] = to_s
        w_sum[k] = to_e + to_w + to_n + to_s + w_z[k] + w_z[k + 1]

    def operator(vp, k):
        here = vp[k, TOP:END, :]
        edge = halo[k]
        lower = vp[jnp.maximum(k - 1, 0), TOP:END, :]
        upper = vp[jnp.minimum(k + 1, NZ - 1), TOP:END, :]
        out = w_sum[k] * here - w_e[k] * east(here, edge) - w_w[k] * west(here, edge)
        out = out - w_n[k] * vp[k, TOP - 1 : END - 1, :] - w_s[k] * vp[k, TOP + 1 : END + 1, :]
        return out - w_z[k] * lower - w_z[k + 1] * upper

    def fold(values):
        part = values.reshape(values.shape[0] // 8, 8, values.shape[1]).sum(0)
        out = part[:, :128]
        for c in range(128, values.shape[1], 128):
            out = out + part[:, c : c + 128]
        return out

    load_b.wait()
    for t in far + [0]:
        k = lax.rem(p + t, NZ)
        value = res[k] - operator(vp_x, k)
        res[k] = value
        if t:
            xsend[k] = value.astype(BF16)
            remote(
                xsend.at[k], xrecv.at[p], a2a_send.at[0, 0], a2a_recv.at[0, 0], {"px": k}
            ).start()
        else:
            xrecv[p] = value.astype(BF16)
    sent_later(xsend.at[pl.ds(0, PX - 1)], a2a_send.at[0, 0])

    for t in far:
        k = lax.rem(p + t, PX)
        remote(
            cls_send.at[k], cls_recv.at[1, p], cls_sem.at[0, 1], cls_sem.at[1, 1], {"px": k}
        ).start()
    cls_recv[1, p] = cls_send[p]
    sent_later(cls_recv.at[1, pl.ds(0, PX - 1)], cls_sem.at[0, 1])

    load_v.wait()

    half_lane = lane((32, 128)) < 64

    def product(ref, cols):
        return jnp.dot(ref[...], vec[:, cols], preferred_element_type=F32)

    def scatter_tile(src, dst, it, which, t, g):
        for u in range(4):
            if t == 0 and u == 0:
                dst[it, q] = src[it, q]
                continue
            dest = g * 4 + (lax.rem(q + u, 4) if t == 0 else u)
            remote(
                src.at[it, dest], dst.at[it, q], a2a_send.at[it, which], a2a_recv.at[it, which], {"py": dest}
            ).start()

    def x_forward(it):
        for t in list(range(1, G)) + [0]:
            g = lax.rem(q // 4 + t, G)
            tile = product(lhs, block(g, 256))
            turned = jnp.concatenate([tile[:, :128], tile[:, 128:]], axis=0).T
            ysend[it, block(g, 4)] = turned.astype(BF16).reshape(4, 32, 128)
            scatter_tile(ysend, yrecv, it, 1, t, g)
        sent_later(ysend.at[it, pl.ds(0, PY - 1)], a2a_send.at[it, 1])

    def y_arrive(it):
        await_bytes(yrecv.at[it, pl.ds(0, PY - 1)], a2a_recv.at[it, 1])
        for m in range(PY // 2):
            even, odd = yrecv[it, 2 * m].astype(F32), yrecv[it, 2 * m + 1].astype(F32)
            low = jnp.where(half_lane, even, pltpu.roll(odd, 64, 1))
            high = jnp.where(half_lane, pltpu.roll(even, 64, 1), odd)
            lhs[0:32, m * 128 : (m + 1) * 128] = low.astype(BF16)
            lhs[32:64, m * 128 : (m + 1) * 128] = high.astype(BF16)

    def spectral(it, alpha):
        acc = jnp.zeros((8, 128), F32)
        for t in range(G):
            cols = slice(t * 256, (t + 1) * 256)
            tile = product(lhs, cols)
            if it == 0:
                s2[:, cols] = tile
            else:
                tile = s2[:, cols] - alpha * tile
            scaled = (tile * dinv[:, cols]).astype(BF16)
            s3[:, cols] = scaled
            acc = acc + fold(tile * scaled.astype(F32))
        return acc

    def y_back(it):
        for t in list(range(1, G)) + [0]:
            g = lax.rem(q // 4 + t, G)
            tile = product(s3, block(g, 256))
            for h in range(2):
                low, high = tile[0:32, h * 128 : h * 128 + 128], tile[32:64, h * 128 : h * 128 + 128]
                even = jnp.where(half_lane, low, pltpu.roll(high, 64, 1))
                odd = jnp.where(half_lane, pltpu.roll(low, 64, 1), high)
                zsend[it, g * 4 + 2 * h] = even.astype(BF16)
                zsend[it, g * 4 + 2 * h + 1] = odd.astype(BF16)
            scatter_tile(zsend, zrecv, it, 2, t, g)
        sent_later(zsend.at[it, pl.ds(0, PY - 1)], a2a_send.at[it, 2])

    def z_arrive(it):
        await_bytes(zrecv.at[it, pl.ds(0, PY - 1)], a2a_recv.at[it, 2])
        for g in range(G):
            turned = zrecv[it, 4 * g : 4 * g + 4].reshape(128, 128).astype(F32).T.astype(BF16)
            lhs[:, g * 256 : g * 256 + 128] = turned[0:64]
            lhs[:, g * 256 + 128 : g * 256 + 256] = turned[64:128]

    def line_copies(h):
        return [
            remote(row_send.at[h, 0], row_recv.at[h, 1], line_send.at[h, 0], line_recv.at[h, 0], north),
            remote(row_send.at[h, 1], row_recv.at[h, 0], line_send.at[h, 1], line_recv.at[h, 1], south),
        ]

    def x_back(it):
        for c in range(PX):
            tile = product(lhs, slice(c * XL, (c + 1) * XL)).astype(BF16)
            bsend[it, c] = tile
            zp[it, TOP:END, c * XL : (c + 1) * XL] = tile.astype(F32)
            remote(
                bsend.at[it, c], above.at[it, c], line_send.at[it, 2], line_recv.at[it, 2], west_of
            ).start()
            remote(
                bsend.at[it, c], below.at[it, c], line_send.at[it, 3], line_recv.at[it, 3], east_of
            ).start()
        row_send[it, 0] = zp[it, TOP : TOP + 1, :]
        row_send[it, 1] = zp[it, END - 1 : END, :]
        rows = start(line_copies(it))
        sent_later(bsend.at[it], line_send.at[it, 2])
        sent_later(bsend.at[it], line_send.at[it, 3])
        return rows

    def edges(it):
        r, l = row((8 * PX, XL)), lane((8 * PX, XL))
        out = jnp.zeros((8 * PX, ROWS), F32)
        for c in range(PX):
            hot = ((r == 8 * c + 8) & (l == XL - 1)) | ((r == 8 * c - 7) & (l == 0))
            out = out + lax.dot_general(
                jnp.where(hot, 1.0, 0.0).astype(BF16), bsend[it, c], NT, preferred_element_type=F32
            )
        edge_send[it] = out.reshape(PX, 8, ROWS)

    def to_grid(it):
        for c in range(PX):
            cols = slice(c * XL, (c + 1) * XL)
            hrow_send[it, c, 0] = zp[it, TOP - 1 : TOP, cols]
            hrow_send[it, c, 1] = zp[it, END : END + 1, cols]
        trio = (
            (bsend, brecv, a2a_send.at[it, 3], a2a_recv.at[it, 3]),
            (hrow_send, hrow_recv, grid_send.at[it, 0], grid_recv.at[it, 0]),
            (edge_send, edge_recv, grid_send.at[it, 1], grid_recv.at[it, 1]),
        )
        for t in far:
            c = lax.rem(p + t, PX)
            for src, dst, send, recv in trio:
                remote(src.at[it, c], dst.at[it, p], send, recv, {"px": c}).start()
        for src, dst, send, recv in trio:
            dst[it, p] = src[it, p]
            sent_later(src.at[it, pl.ds(0, PX - 1)], send)

    def grid_arrive(it):
        for dst, recv in (
            (brecv, a2a_recv.at[it, 3]),
            (hrow_recv, grid_recv.at[it, 0]),
            (edge_recv, grid_recv.at[it, 1]),
        ):
            await_bytes(dst.at[it, pl.ds(0, PX - 1)], recv)

    def plane_copies():
        return [
            remote(cls_recv.at[1], cls_recv.at[2], cls_sem.at[0, 2], cls_sem.at[1, 2], west_of),
            remote(cls_recv.at[1], cls_recv.at[0], cls_sem.at[0, 0], cls_sem.at[1, 0], east_of),
        ]

    def pencil_coefficients():
        await_bytes(cls_recv.at[1, pl.ds(0, PX - 1)], cls_sem.at[1, 1])
        planes = start(plane_copies())

        @pl.loop(0, PX)
        def _(c):
            pc[TOP:END, block(c, XL)] = lookup(cls_recv[1, c].astype(F32))

        row_send[2, 0] = pc[TOP : TOP + 1, :]
        row_send[2, 1] = pc[END - 1 : END, :]
        return planes + start(line_copies(2))

    wide = lane((16, N))

    def pencil_weights(rows):
        wait_all(rows)

        @pl.loop(0, PX)
        def _(c):
            cols = block(c, XL)
            here = pc[TOP:END, cols]
            p_d[:, cols] = 0.5 * has_first * (here + lookup(cls_recv[0, c].astype(F32)))
            p_u[:, cols] = 0.5 * has_last * (here + lookup(cls_recv[2, c].astype(F32)))

        pc[TOP - 1 : TOP, :] = row_recv[2, 0] * has_north
        pc[END : END + 1, :] = row_recv[2, 1] * has_south
        for r in range(0, ROWS, 16):
            at = slice(r, r + 16)
            here = pc[TOP + r : TOP + r + 16, :]
            to_e = 0.5 * (here + jnp.where(wide == N - 1, 0.0, pltpu.roll(here, N - 1, 1)))
            to_w = 0.5 * (here + jnp.where(wide == 0, 0.0, pltpu.roll(here, 1, 1)))
            to_n = 0.5 * (here + pc[TOP - 1 + r : TOP + 15 + r, :])
            to_s = 0.5 * (here + pc[TOP + 1 + r : TOP + 17 + r, :])
            p_e[at, :] = jnp.where(wide == N - 1, 0.0, to_e)
            p_w[at, :] = jnp.where(wide == 0, 0.0, to_w)
            p_n[at, :] = to_n
            p_s[at, :] = to_s
            p_sum[at, :] = to_e + to_w + to_n + to_s + p_u[at, :] + p_d[at, :]

    def beside(ref, it, r):
        return jnp.concatenate([ref[it, c, r : r + 16, :] for c in range(PX)], axis=1).astype(F32)

    def pencil_operator(it, rows, beta):
        edges(it)
        wait_all(rows)
        zp[it, TOP - 1 : TOP, :] = row_recv[it, 0] * has_north
        zp[it, END : END + 1, :] = row_recv[it, 1] * has_south
        await_bytes(above.at[it], line_recv.at[it, 2])
        await_bytes(below.at[it], line_recv.at[it, 3])
        to_grid(it)
        if it == 1:
            for r in range(0, ROWS + 16, 16):
                if r == 0:
                    at = slice(TOP - 1, 16)
                elif r == ROWS:
                    at = slice(ROWS, END + 1)
                else:
                    at = slice(r, r + 16)
                zp[1, at, :] = zp[1, at, :] + beta * zp[0, at, :]
        acc = jnp.zeros((8, 128), F32)
        for r in range(0, ROWS, 16):
            at = slice(r, r + 16)
            here = zp[it, TOP + r : TOP + r + 16, :]
            up, down = beside(above, it, r), beside(below, it, r)
            if it == 1:
                up = up + beta * beside(above, 0, r)
                down = down + beta * beside(below, 0, r)
            out = p_sum[at, :] * here - p_e[at, :] * pltpu.roll(here, N - 1, 1)
            out = out - p_w[at, :] * pltpu.roll(here, 1, 1)
            out = out - p_n[at, :] * zp[it, TOP - 1 + r : TOP + 15 + r, :]
            out = out - p_s[at, :] * zp[it, TOP + 1 + r : TOP + 17 + r, :]
            out = out - p_u[at, :] * up - p_d[at, :] * down
            if it == 0:
                lhs[at, :] = out.astype(BF16)
            acc = acc + fold(here * out)
        return acc

    def reduce_start(a, first, second_part):
        mine = jnp.concatenate(
            [first.sum(0, keepdims=True), second_part.sum(0, keepdims=True)], axis=1
        )
        ary_send[a, 0] = mine
        ary[a, q] = mine

        @pl.loop(1, PY)
        def _(t):
            dest = lax.rem(q + t, PY)
            remote(
                ary_send.at[a, 0], ary.at[a, q], ar_send.at[a, 1], ar_recv.at[a, 1], {"py": dest}
            ).start()

        sent_later(ary.at[a, pl.ds(0, PY - 1)], ar_send.at[a, 1])

    def reduce_middle(a):
        await_bytes(ary.at[a, pl.ds(0, PY - 1)], ar_recv.at[a, 1])
        mine = ary[a, 0]
        for t in range(1, PY):
            mine = mine + ary[a, t]
        arx_send[a, 0] = mine
        arx[a, p] = mine
        for t in far:
            dest = lax.rem(p + t, PX)
            remote(
                arx_send.at[a, 0], arx.at[a, p], ar_send.at[a, 0], ar_recv.at[a, 0], {"px": dest}
            ).start()
        sent_later(arx.at[a, pl.ds(0, PX - 1)], ar_send.at[a, 0])

    def reduce_end(a):
        await_bytes(arx.at[a, pl.ds(0, PX - 1)], ar_recv.at[a, 0])
        total = arx[a, 0]
        for t in range(1, PX):
            total = total + arx[a, t]
        return (
            total[:, :128].sum(1, keepdims=True),
            total[:, 128:].sum(1, keepdims=True),
        )

    zero = jnp.zeros((8, 128), F32)

    place_r, place_l = row((8, XL)), lane((8, XL))
    outside = jnp.where(
        ((place_r == 0) & (place_l == 0)) | ((place_r == 1) & (place_l == XL - 1)), 1.0, 0.0
    )

    def grid_direction(it, vp, beta):
        def mixed(ref, k):
            return ref[0, k] if it == 0 else ref[1, k] + beta * ref[0, k]

        for k in range(NZ):
            around = mixed(hrow_recv, k)
            vp[k, TOP - 1 : TOP, :] = around[0]
            vp[k, END : END + 1, :] = around[1]
            halo[k] = lax.dot_general(
                mixed(edge_recv, k), outside, TN, precision=HIGH, preferred_element_type=F32
            )

        @pl.loop(0, NZ)
        def _(k):
            value = brecv[it, k].astype(F32)
            if it == 1:
                value = value + beta * vp_0[k, TOP:END, :]
                direction[k] = value
            vp[k, TOP:END, :] = value

    await_bytes(xrecv.at[pl.ds(0, PX - 1)], a2a_recv.at[0, 0])
    for c in range(PX):
        lhs[:, c * XL : (c + 1) * XL] = xrecv[c]
    x_forward(0)
    coeff_rows = pencil_coefficients()
    y_arrive(0)
    gamma_part = spectral(0, None)
    y_back(0)
    pencil_weights(coeff_rows)
    z_arrive(0)
    rows = x_back(0)
    curve = pencil_operator(0, rows, None)
    reduce_start(0, gamma_part, curve)

    x_forward(1)
    reduce_middle(0)
    grid_arrive(0)
    grid_direction(0, vp_0, None)

    @pl.loop(0, NZ)
    def _(k):
        image[k] = operator(vp_0, k)

    y_arrive(1)
    gamma0, curve0 = reduce_end(0)
    alpha0 = gamma0 / curve0
    reduce_start(1, spectral(1, alpha0), zero)
    y_back(1)

    @pl.loop(0, NZ)
    def _(k):
        res[k] = res[k] - alpha0 * image[k]
        sol[k] = vp_x[k, TOP:END, :] + alpha0 * vp_0[k, TOP:END, :]

    store_x = pltpu.make_async_copy(sol, sol_hbm, store_sem.at[0])
    store_r = pltpu.make_async_copy(res, res_hbm, store_sem.at[1])
    store_x.start()
    store_r.start()
    reduce_middle(1)
    z_arrive(1)
    rows = x_back(1)
    gamma1, _ = reduce_end(1)
    beta = gamma1 / gamma0
    reduce_start(2, pencil_operator(1, rows, beta), zero)

    reduce_middle(2)
    grid_arrive(1)
    grid_direction(1, vp_1, beta)
    store_d = pltpu.make_async_copy(direction, dir_hbm, store_sem.at[2])
    store_d.start()

    @pl.loop(0, NZ)
    def _(k):
        image[k] = operator(vp_1, k)

    store_i = pltpu.make_async_copy(image, image_hbm, store_sem.at[3])
    store_i.start()
    curve1, _ = reduce_end(2)
    alpha_out[...] = jnp.broadcast_to(gamma1 / curve1, (1, 128))
    store_a = pltpu.make_async_copy(alpha_out, alpha_hbm, store_sem.at[4])
    store_a.start()

    for wait in pending:
        wait()
    store_x.wait()
    store_r.wait()
    store_d.wait()
    store_i.wait()
    store_a.wait()


def last_update(alpha, x, r, d, image, sol, res, direction):
    step = alpha[0:1, 0:1]
    sol[...] = x[...] + step * d[...]
    res[...] = r[...] - step * image[...]
    direction[...] = d[...]


def shards(PX, PY, right_side, solution_in, classes, coeff_table, eigenvectors, eigenvalues, level_shift):
    XL, N = right_side.shape[2], eigenvectors.shape[0]
    out = jax.ShapeDtypeStruct(right_side.shape, F32)
    hbm = pl.BlockSpec(memory_space=pl.ANY)
    buffers = scratch(PX, PY, XL, N)
    x, r, d, image, alpha = pl.pallas_call(
        functools.partial(kernel, PX, PY, tuple(buffers)),
        out_shape=[out] * 4 + [jax.ShapeDtypeStruct((1, 128), F32)],
        in_specs=[hbm] * 7,
        out_specs=[hbm] * 5,
        scratch_shapes=list(buffers.values()),
        compiler_params=pltpu.CompilerParams(
            collective_id=0, has_side_effects=True, vmem_limit_bytes=60 * 2**20
        ),
    )(
        right_side,
        solution_in,
        classes,
        coeff_table,
        eigenvectors,
        eigenvalues.reshape(1, N),
        level_shift,
    )
    levels = pl.BlockSpec((2, ROWS, XL), lambda k: (k, 0, 0))
    return tuple(
        pl.pallas_call(
            last_update,
            grid=(PX // 2,),
            out_shape=[out] * 3,
            in_specs=[pl.BlockSpec((1, 128), lambda k: (0, 0))] + [levels] * 4,
            out_specs=[levels] * 3,
        )(alpha, x, r, d, image)
    )


def solution(mesh):
    field = P(None, "py", "px")
    return jax.shard_map(
        functools.partial(shards, mesh.shape["px"], mesh.shape["py"]),
        mesh=mesh,
        in_specs=(field, field, field, P(), P(), P(), P()),
        out_specs=(field, field, field),
        check_vma=False,
    )
```

```python
import functools

import jax
import jax.numpy as jnp
from jax import lax
from jax.experimental import pallas as pl
from jax.experimental.pallas import tpu as pltpu
from jax.sharding import PartitionSpec as P

F32 = jnp.float32
BF16 = jnp.bfloat16
ROWS = 64
TOP, END = 8, 8 + ROWS
HIGH = lax.Precision.HIGHEST
NT = (((1,), (1,)), ((), ()))
TN = (((0,), (0,)), ((), ()))


def scratch(PX, PY, XL, N):
    NZ = PX
    field = pltpu.VMEM((NZ, ROWS, XL), F32)
    padded = pltpu.VMEM((NZ, ROWS + 16, XL), F32)
    lines = pltpu.VMEM((ROWS, N), F32)
    padded_lines = pltpu.VMEM((ROWS + 16, N), F32)
    tiles = pltpu.VMEM((2, PY, 32, 128), BF16)
    dma = pltpu.SemaphoreType.DMA
    return dict(
        vec=pltpu.VMEM((N, N), BF16),
        eig=pltpu.VMEM((1, N), F32),
        table=pltpu.SMEM((16,), F32),
        shift=pltpu.SMEM((NZ,), F32),
        cls=pltpu.VMEM((NZ, ROWS, XL), jnp.int32),
        sol=field,
        res=field,
        direction=field,
        image=field,
        vp_x=padded,
        vp_0=padded,
        vp_1=padded,
        cp=padded,
        halo=field,
        chalo=field,
        w_e=field,
        w_w=field,
        w_s=field,
        w_n=field,
        w_z=pltpu.VMEM((NZ + 1, ROWS, XL), F32),
        w_sum=field,
        cls_send=pltpu.VMEM((NZ, ROWS, XL), BF16),
        cls_recv=pltpu.VMEM((3, PX, ROWS, XL), BF16),
        pc=padded_lines,
        p_e=lines,
        p_w=lines,
        p_s=lines,
        p_n=lines,
        p_u=lines,
        p_d=lines,
        p_sum=lines,
        zp=pltpu.VMEM((2, ROWS + 16, N), F32),
        above=pltpu.VMEM((2, PX, ROWS, XL), BF16),
        below=pltpu.VMEM((2, PX, ROWS, XL), BF16),
        row_send=pltpu.VMEM((3, 2, 1, N), F32),
        row_recv=pltpu.VMEM((3, 2, 1, N), F32),
        xsend=pltpu.VMEM((PX, ROWS, XL), BF16),
        xrecv=pltpu.VMEM((PX, ROWS, XL), BF16),
        ysend=tiles,
        yrecv=tiles,
        zsend=tiles,
        zrecv=tiles,
        bsend=pltpu.VMEM((2, PX, ROWS, XL), BF16),
        brecv=pltpu.VMEM((2, PX, ROWS, XL), BF16),
        lhs=pltpu.VMEM((ROWS, N), BF16),
        acc=lines,
        inner=lines,
        image_0=lines,
        s2=lines,
        s3=pltpu.VMEM((ROWS, N), BF16),
        dinv=lines,
        eigc=pltpu.VMEM((128, 128), F32),
        rsend=pltpu.VMEM((1, 2, 2 * NZ, XL), F32),
        rrecv=pltpu.VMEM((1, 2, 2 * NZ, XL), F32),
        csend=pltpu.VMEM((1, 8, NZ * ROWS), F32),
        crecv=pltpu.VMEM((1, 16, NZ * ROWS), F32),
        hrow_send=pltpu.VMEM((2, PX, 2, 1, XL), F32),
        hrow_recv=pltpu.VMEM((2, PX, 2, 1, XL), F32),
        edge_send=pltpu.VMEM((2, PX, 8, ROWS), F32),
        edge_recv=pltpu.VMEM((2, PX, 8, ROWS), F32),
        alpha_out=pltpu.VMEM((1, 128), F32),
        arx_send=pltpu.VMEM((3, 1, 1, 256), F32),
        arx=pltpu.VMEM((3, PX, 1, 256), F32),
        ary_send=pltpu.VMEM((3, 1, 1, 256), F32),
        ary=pltpu.VMEM((3, PY, 1, 256), F32),
        load_sem=dma((7,)),
        store_sem=dma((5,)),
        halo_send=dma((1, 4)),
        halo_recv=dma((1, 4)),
        grid_send=dma((2, 2)),
        grid_recv=dma((2, 2)),
        cls_sem=dma((2, 3)),
        line_send=dma((3, 4)),
        line_recv=dma((3, 4)),
        a2a_send=dma((2, 4)),
        a2a_recv=dma((2, 4, 8)),
        ar_send=dma((3, 2)),
        ar_recv=dma((3, 2)),
    )


def kernel(PX, PY, names, *refs):
    b_hbm, x_hbm, cls_hbm, table_hbm, vec_hbm, eig_hbm, shift_hbm = refs[:7]
    sol_hbm, res_hbm, dir_hbm, image_hbm, alpha_hbm = refs[7:12]
    R = dict(zip(names, refs[12:]))
    vec, eig, table, shift, cls = (R[n] for n in ("vec", "eig", "table", "shift", "cls"))
    sol, res, direction, image = (R[n] for n in ("sol", "res", "direction", "image"))
    vp_x, vp_0, vp_1, cp, halo, chalo = (R[n] for n in ("vp_x", "vp_0", "vp_1", "cp", "halo", "chalo"))
    w_e, w_w, w_s, w_n, w_z, w_sum = (R[n] for n in ("w_e", "w_w", "w_s", "w_n", "w_z", "w_sum"))
    p_e, p_w, p_s, p_n, p_u, p_d, p_sum = (
        R[n] for n in ("p_e", "p_w", "p_s", "p_n", "p_u", "p_d", "p_sum")
    )
    cls_send, cls_recv, pc, zp = (R[n] for n in ("cls_send", "cls_recv", "pc", "zp"))
    above, below, row_send, row_recv = (R[n] for n in ("above", "below", "row_send", "row_recv"))
    xsend, xrecv, ysend, yrecv = (R[n] for n in ("xsend", "xrecv", "ysend", "yrecv"))
    zsend, zrecv, bsend, brecv = (R[n] for n in ("zsend", "zrecv", "bsend", "brecv"))
    lhs, s2, s3, dinv, eigc = (R[n] for n in ("lhs", "s2", "s3", "dinv", "eigc"))
    acc, inner, image_0 = (R[n] for n in ("acc", "inner", "image_0"))
    rsend, rrecv, csend, crecv = (R[n] for n in ("rsend", "rrecv", "csend", "crecv"))
    hrow_send, hrow_recv, edge_send, edge_recv, grid_send, grid_recv, alpha_out = (
        R[n]
        for n in (
            "hrow_send",
            "hrow_recv",
            "edge_send",
            "edge_recv",
            "grid_send",
            "grid_recv",
            "alpha_out",
        )
    )
    arx_send, arx, ary_send, ary = (R[n] for n in ("arx_send", "arx", "ary_send", "ary"))
    load_sem, store_sem, halo_send, halo_recv = (
        R[n] for n in ("load_sem", "store_sem", "halo_send", "halo_recv")
    )
    cls_sem, line_send, line_recv = (R[n] for n in ("cls_sem", "line_send", "line_recv"))
    a2a_send, a2a_recv, ar_send, ar_recv = (
        R[n] for n in ("a2a_send", "a2a_recv", "ar_send", "ar_recv")
    )

    NZ, XL, N = PX, image.shape[2], vec.shape[0]
    G = N // 256
    p, q = lax.axis_index("px"), lax.axis_index("py")
    pending = []
    far = sorted(range(1, PX), key=lambda t: -min(t, PX - t))
    far_groups = sorted(range(G), key=lambda t: -min(t, G - t))

    def lane(shape):
        return lax.broadcasted_iota(jnp.int32, shape, len(shape) - 1)

    def row(shape):
        return lax.broadcasted_iota(jnp.int32, shape, len(shape) - 2)

    def block(i, size):
        return pl.ds(pl.multiple_of(i * size, size), size)

    def remote(src, dst, send, recv, where):
        return pltpu.make_async_remote_copy(
            src_ref=src, dst_ref=dst, send_sem=send, recv_sem=recv, device_id=where
        )

    def await_bytes(ref, sem):
        pltpu.make_async_copy(ref, ref, sem).wait()

    def sent_later(ref, sem):
        pending.append(lambda: await_bytes(ref, sem))

    north = {"py": lax.rem(q + PY - 1, PY)}
    south = {"py": lax.rem(q + 1, PY)}
    west_of = {"px": lax.rem(p + PX - 1, PX)}
    east_of = {"px": lax.rem(p + 1, PX)}
    has_north = jnp.where(q > 0, 1.0, 0.0).astype(F32)
    has_south = jnp.where(q < PY - 1, 1.0, 0.0).astype(F32)
    has_first = jnp.where(p > 0, 1.0, 0.0).astype(F32)
    has_last = jnp.where(p < PX - 1, 1.0, 0.0).astype(F32)

    load_cls = pltpu.make_async_copy(cls_hbm, cls, load_sem.at[0])
    load_x = pltpu.make_async_copy(x_hbm, vp_x.at[:, TOP:END, :], load_sem.at[1])
    load_b = pltpu.make_async_copy(b_hbm, res, load_sem.at[2])
    load_v = pltpu.make_async_copy(vec_hbm, vec, load_sem.at[3])
    load_t = pltpu.make_async_copy(table_hbm, table, load_sem.at[4])
    load_s = pltpu.make_async_copy(shift_hbm, shift, load_sem.at[5])
    load_e = pltpu.make_async_copy(eig_hbm, eig, load_sem.at[6])
    for load in (load_x, load_cls, load_t, load_s, load_e, load_b, load_v):
        load.start()

    barrier = pltpu.get_barrier_semaphore()

    @pl.loop(1, PX)
    def _(t):
        pl.semaphore_signal(barrier, inc=1, device_id={"px": lax.rem(p + t, PX)})

    @pl.loop(1, PY)
    def _(t):
        pl.semaphore_signal(barrier, inc=1, device_id={"py": lax.rem(q + t, PY)})

    def pick(base, kind, rows):
        r, l = row((rows, XL)), lane((rows, XL))
        hot = ((r == base) & (l == 0)) | ((r == base + 1) & (l == XL - 1))
        return jnp.where(hot, 1.0, 0.0).astype(kind)

    def place(base):
        r, l = row((16, XL)), lane((16, XL))
        hot_l = jnp.where((r == base + 1) & (l == 0), has_first, 0.0)
        hot_r = jnp.where((r == 8 + base) & (l == XL - 1), has_last, 0.0)
        return hot_l + hot_r

    def lookup(values):
        picks = values.astype(jnp.int32)
        level = [table[label] for label in range(16)]
        for bit in range(4):
            odd = (picks & (1 << bit)) != 0
            level = [jnp.where(odd, level[i + 1], level[i]) for i in range(0, len(level), 2)]
        return level[0]

    def halo_copies(h):
        return [
            remote(rsend.at[h, 0], rrecv.at[h, 1], halo_send.at[h, 0], halo_recv.at[h, 0], north),
            remote(rsend.at[h, 1], rrecv.at[h, 0], halo_send.at[h, 1], halo_recv.at[h, 1], south),
            remote(csend.at[h], crecv.at[h, pl.ds(8, 8)], halo_send.at[h, 2], halo_recv.at[h, 2], west_of),
            remote(csend.at[h], crecv.at[h, pl.ds(0, 8)], halo_send.at[h, 3], halo_recv.at[h, 3], east_of),
        ]

    def start(copies):
        for copy in copies:
            copy.start()
            pending.append(copy.wait_send)
        return copies

    load_x.wait()
    load_cls.wait()
    for k in range(NZ):
        rsend[0, 0, k : k + 1, :] = vp_x[k, TOP : TOP + 1, :]
        rsend[0, 1, k : k + 1, :] = vp_x[k, END - 1 : END, :]
        rsend[0, 0, NZ + k : NZ + k + 1, :] = cls[k, 0:1, :].astype(F32)
        rsend[0, 1, NZ + k : NZ + k + 1, :] = cls[k, ROWS - 1 : ROWS, :].astype(F32)
    x_flat = vp_x[:, TOP:END, :].reshape(NZ * ROWS, XL)
    cls_flat = cls[...].reshape(NZ * ROWS, XL).astype(F32).astype(BF16)
    csend[0] = (
        lax.dot_general(pick(0, BF16, 16), x_flat.astype(BF16), NT, preferred_element_type=F32)
        + lax.dot_general(pick(2, BF16, 16), cls_flat, NT, preferred_element_type=F32)
    )[0:8]
    cls_send[...] = cls_flat.reshape(NZ, ROWS, XL)
    load_t.wait()
    load_s.wait()
    load_e.wait()
    pl.semaphore_wait(barrier, PX - 1 + PY - 1)
    copies = start(halo_copies(0))

    @pl.loop(0, NZ)
    def _(k):
        cp[k, TOP:END, :] = lookup(cls[k])

    w_z[0] = jnp.zeros((ROWS, XL), F32)
    w_z[NZ] = jnp.zeros((ROWS, XL), F32)

    @pl.loop(0, NZ - 1)
    def _(k):
        w_z[k + 1] = 0.5 * (cp[k, TOP:END, :] + cp[k + 1, TOP:END, :])

    def wait_all(copies):
        for copy in copies:
            copy.wait_recv()

    def fill_rows(h, vp):
        for k in range(NZ):
            vp[k, TOP - 1 : TOP, :] = rrecv[h, 0, k : k + 1, :] * has_north
            vp[k, END : END + 1, :] = rrecv[h, 1, k : k + 1, :] * has_south

    wait_all(copies)
    fill_rows(0, vp_x)
    north_row = lookup(rrecv[0, 0, NZ : 2 * NZ, :]) * has_north
    south_row = lookup(rrecv[0, 1, NZ : 2 * NZ, :]) * has_south
    for k in range(NZ):
        cp[k, TOP - 1 : TOP, :] = north_row[k : k + 1]
        cp[k, END : END + 1, :] = south_row[k : k + 1]

    def columns(values, base):
        high = values.astype(BF16)
        rest = values - high.astype(F32)
        middle = rest.astype(BF16)
        low = (rest - middle.astype(F32)).astype(BF16)
        hot = place(base).astype(BF16)
        out = lax.dot_general(
            jnp.concatenate([high, middle, low], axis=0),
            jnp.concatenate([hot, hot, hot], axis=0),
            TN,
            preferred_element_type=F32,
        )
        return out.reshape(NZ, ROWS, XL)

    halo[...] = columns(crecv[0], 0)
    chalo[...] = columns(lookup(crecv[0]), 2)

    lanes = lane((ROWS, XL))

    def east(values, edge):
        return jnp.where(lanes == XL - 1, edge, pltpu.roll(values, XL - 1, 1))

    def west(values, edge):
        return jnp.where(lanes == 0, edge, pltpu.roll(values, 1, 1))

    @pl.loop(0, NZ)
    def _(k):
        here = cp[k, TOP:END, :]
        edge = chalo[k]
        to_e = 0.5 * (here + east(here, edge))
        to_w = 0.5 * (here + west(here, edge))
        to_n = 0.5 * (here + cp[k, TOP - 1 : END - 1, :])
        to_s = 0.5 * (here + cp[k, TOP + 1 : END + 1, :])
        w_e[k] = to_e
        w_w[k] = to_w
        w_n[k] = to_n
        w_s[k] = to_s
        w_sum[k] = to_e + to_w + to_n + to_s + w_z[k] + w_z[k + 1]

    def operator(vp, k):
        here = vp[k, TOP:END, :]
        edge = halo[k]
        lower = vp[jnp.maximum(k - 1, 0), TOP:END, :]
        upper = vp[jnp.minimum(k + 1, NZ - 1), TOP:END, :]
        out = w_sum[k] * here - w_e[k] * east(here, edge) - w_w[k] * west(here, edge)
        out = out - w_n[k] * vp[k, TOP - 1 : END - 1, :] - w_s[k] * vp[k, TOP + 1 : END + 1, :]
        return out - w_z[k] * lower - w_z[k + 1] * upper

    def fold(values):
        part = values.reshape(values.shape[0] // 8, 8, values.shape[1]).sum(0)
        out = part[:, :128]
        for c in range(128, values.shape[1], 128):
            out = out + part[:, c : c + 128]
        return out

    load_b.wait()
    for t in far + [0]:
        k = lax.rem(p + t, NZ)
        value = res[k] - operator(vp_x, k)
        res[k] = value
        if t:
            xsend[k] = value.astype(BF16)
            remote(
                xsend.at[k], xrecv.at[p], a2a_send.at[0, 0], a2a_recv.at[0, 0, p], {"px": k}
            ).start()
        else:
            xrecv[p] = value.astype(BF16)
    sent_later(xsend.at[pl.ds(0, PX - 1)], a2a_send.at[0, 0])

    group, part = q // 4, lax.rem(q, 4)
    for half in range(2):
        cols = pl.ds(pl.multiple_of(group * 256 + half * 128, 128), 128)
        eigc[...] = jnp.broadcast_to(eig[:, cols], (128, 128)).T
        mine = eigc[block(part, 32), 0:1] + shift[p]
        dinv[half * 32 : half * 32 + 32, :] = 1.0 / (mine + eig[...])

    load_v.wait()

    half_lane = lane((32, 128)) < 64
    own_group = q // 4

    def product(ref, rows, cols):
        return jnp.dot(ref[:, rows], vec[rows, cols], preferred_element_type=F32)

    def in_steps(parts, size, fetch, consume, order):
        steps = [parts[i : i + 2] for i in range(0, len(parts), 2)]
        for i, step in enumerate(steps):
            rows = [block(fetch(t), size) for t in step]
            for n in order:
                cols = block(n, 256)
                tile = product(lhs, rows[0], cols)
                for r in rows[1:]:
                    tile = tile + product(lhs, r, cols)
                if i:
                    tile = acc[:, cols] + tile
                if i == len(steps) - 1:
                    consume(n, tile)
                else:
                    acc[:, cols] = tile

    def scatter_tile(src, dst, it, which, t, g):
        for u in range(4):
            if t == 0 and u == 0:
                dst[it, q] = src[it, q]
                continue
            dest = g * 4 + (lax.rem(q + u, 4) if t == 0 else u)
            remote(
                src.at[it, dest],
                dst.at[it, q],
                a2a_send.at[it, which],
                a2a_recv.at[it, which, own_group],
                {"py": dest},
            ).start()

    def await_group(dst, it, which, t):
        g = lax.rem(own_group + G - t, G)
        await_bytes(dst.at[it, pl.ds(0, 4 if t else 3)], a2a_recv.at[it, which, g])
        return g

    groups = [lax.rem(own_group + t, G) for t in far_groups]

    def fetch_x(t):
        c = lax.rem(p + PX - t, PX)
        if t:
            await_bytes(xrecv.at[0], a2a_recv.at[0, 0, c])
        lhs[:, block(c, XL)] = xrecv[c]
        return c

    def x_forward(it):
        def turn(i, g, tile):
            turned = jnp.concatenate([tile[:, :128], tile[:, 128:]], axis=0).T
            ysend[it, block(g, 4)] = turned.astype(BF16).reshape(4, 32, 128)
            scatter_tile(ysend, yrecv, it, 1, far_groups[i], g)

        if it == 0:
            count = iter(range(G))
            in_steps([0] + far, XL, fetch_x, lambda g, tile: turn(next(count), g, tile), groups)
        else:
            for i, g in enumerate(groups):
                turn(i, g, product(lhs, slice(None), block(g, 256)))
        sent_later(ysend.at[it, pl.ds(0, PY - 1)], a2a_send.at[it, 1])

    def fetch_y(it):
        def fetch(t):
            g = await_group(yrecv, it, 1, t)
            for m in range(2):
                even = yrecv[it, 4 * g + 2 * m].astype(F32)
                odd = yrecv[it, 4 * g + 2 * m + 1].astype(F32)
                low = jnp.where(half_lane, even, pltpu.roll(odd, 64, 1))
                high = jnp.where(half_lane, pltpu.roll(even, 64, 1), odd)
                cols = block(2 * g + m, 128)
                lhs[0:32, cols] = low.astype(BF16)
                lhs[32:64, cols] = high.astype(BF16)
            return g

        return fetch

    def spectral(it, alpha):
        sums = []

        def scale(n, tile):
            cols = block(n, 256)
            if it == 0:
                s2[:, cols] = tile
            else:
                tile = s2[:, cols] - alpha() * tile
            scaled = (tile * dinv[:, cols]).astype(BF16)
            s3[:, cols] = scaled
            sums.append(fold(tile * scaled.astype(F32)))

        in_steps(far_groups, 256, fetch_y(it), scale, range(G))
        return sum(sums[1:], sums[0])

    def y_back(it):
        for i, g in enumerate(groups):
            tile = product(s3, slice(None), block(g, 256))
            for h in range(2):
                low, high = tile[0:32, h * 128 : h * 128 + 128], tile[32:64, h * 128 : h * 128 + 128]
                even = jnp.where(half_lane, low, pltpu.roll(high, 64, 1))
                odd = jnp.where(half_lane, pltpu.roll(low, 64, 1), high)
                zsend[it, g * 4 + 2 * h] = even.astype(BF16)
                zsend[it, g * 4 + 2 * h + 1] = odd.astype(BF16)
            scatter_tile(zsend, zrecv, it, 2, far_groups[i], g)
        sent_later(zsend.at[it, pl.ds(0, PY - 1)], a2a_send.at[it, 2])

    def fetch_z(it):
        def fetch(t):
            g = await_group(zrecv, it, 2, t)
            turned = zrecv[it, block(g, 4)].reshape(128, 128).astype(F32).T.astype(BF16)
            lhs[:, block(2 * g, 128)] = turned[0:64]
            lhs[:, block(2 * g + 1, 128)] = turned[64:128]
            return g

        return fetch

    def line_copies(h):
        return [
            remote(row_send.at[h, 0], row_recv.at[h, 1], line_send.at[h, 0], line_recv.at[h, 0], north),
            remote(row_send.at[h, 1], row_recv.at[h, 0], line_send.at[h, 1], line_recv.at[h, 1], south),
        ]

    def x_back(it):
        def spread(n, tile):
            for c in range(n * 256 // XL, (n + 1) * 256 // XL):
                part = tile[:, c * XL - n * 256 : (c + 1) * XL - n * 256].astype(BF16)
                bsend[it, c] = part
                zp[it, TOP:END, c * XL : (c + 1) * XL] = part.astype(F32)
                for dst, i, where in ((above, 2, west_of), (below, 3, east_of)):
                    remote(
                        bsend.at[it, c], dst.at[it, c], line_send.at[it, i], line_recv.at[it, i], where
                    ).start()

        in_steps(far_groups, 256, fetch_z(it), spread, range(G))
        row_send[it, 0] = zp[it, TOP : TOP + 1, :]
        row_send[it, 1] = zp[it, END - 1 : END, :]
        rows = start(line_copies(it))
        sent_later(bsend.at[it], line_send.at[it, 2])
        sent_later(bsend.at[it], line_send.at[it, 3])
        return rows

    def edges(it):
        r, l = row((8 * PX, XL)), lane((8 * PX, XL))
        out = jnp.zeros((8 * PX, ROWS), F32)
        for c in range(PX):
            hot = ((r == 8 * c + 8) & (l == XL - 1)) | ((r == 8 * c - 7) & (l == 0))
            out = out + lax.dot_general(
                jnp.where(hot, 1.0, 0.0).astype(BF16), bsend[it, c], NT, preferred_element_type=F32
            )
        edge_send[it] = out.reshape(PX, 8, ROWS)

    def to_grid(it):
        for c in range(PX):
            cols = slice(c * XL, (c + 1) * XL)
            hrow_send[it, c, 0] = zp[it, TOP - 1 : TOP, cols]
            hrow_send[it, c, 1] = zp[it, END : END + 1, cols]
        trio = (
            (bsend, brecv, a2a_send.at[it, 3], a2a_recv.at[it, 3, 0]),
            (hrow_send, hrow_recv, grid_send.at[it, 0], grid_recv.at[it, 0]),
            (edge_send, edge_recv, grid_send.at[it, 1], grid_recv.at[it, 1]),
        )
        for t in far:
            c = lax.rem(p + t, PX)
            for src, dst, send, recv in trio:
                remote(src.at[it, c], dst.at[it, p], send, recv, {"px": c}).start()
        for src, dst, send, recv in trio:
            dst[it, p] = src[it, p]
            sent_later(src.at[it, pl.ds(0, PX - 1)], send)

    def grid_arrive(it):
        for dst, recv in (
            (brecv, a2a_recv.at[it, 3, 0]),
            (hrow_recv, grid_recv.at[it, 0]),
            (edge_recv, grid_recv.at[it, 1]),
        ):
            await_bytes(dst.at[it, pl.ds(0, PX - 1)], recv)

    def plane_copies():
        return [
            remote(cls_recv.at[1], cls_recv.at[2], cls_sem.at[0, 2], cls_sem.at[1, 2], west_of),
            remote(cls_recv.at[1], cls_recv.at[0], cls_sem.at[0, 0], cls_sem.at[1, 0], east_of),
        ]

    def send_classes():
        for t in far:
            k = lax.rem(p + t, PX)
            remote(
                cls_send.at[k], cls_recv.at[1, p], cls_sem.at[0, 1], cls_sem.at[1, 1], {"px": k}
            ).start()
        cls_recv[1, p] = cls_send[p]
        sent_later(cls_recv.at[1, pl.ds(0, PX - 1)], cls_sem.at[0, 1])

    def pencil_coefficients():
        await_bytes(cls_recv.at[1, pl.ds(0, PX - 1)], cls_sem.at[1, 1])
        planes = start(plane_copies())

        @pl.loop(0, PX)
        def _(c):
            pc[TOP:END, block(c, XL)] = lookup(cls_recv[1, c].astype(F32))

        row_send[2, 0] = pc[TOP : TOP + 1, :]
        row_send[2, 1] = pc[END - 1 : END, :]
        return planes + start(line_copies(2))

    wide = lane((16, N))

    def pencil_weights(rows):
        wait_all(rows)

        @pl.loop(0, PX)
        def _(c):
            cols = block(c, XL)
            here = pc[TOP:END, cols]
            p_d[:, cols] = 0.5 * has_first * (here + lookup(cls_recv[0, c].astype(F32)))
            p_u[:, cols] = 0.5 * has_last * (here + lookup(cls_recv[2, c].astype(F32)))

        pc[TOP - 1 : TOP, :] = row_recv[2, 0] * has_north
        pc[END : END + 1, :] = row_recv[2, 1] * has_south
        for r in range(0, ROWS, 16):
            at = slice(r, r + 16)
            here = pc[TOP + r : TOP + r + 16, :]
            to_e = 0.5 * (here + jnp.where(wide == N - 1, 0.0, pltpu.roll(here, N - 1, 1)))
            to_w = 0.5 * (here + jnp.where(wide == 0, 0.0, pltpu.roll(here, 1, 1)))
            to_n = 0.5 * (here + pc[TOP - 1 + r : TOP + 15 + r, :])
            to_s = 0.5 * (here + pc[TOP + 1 + r : TOP + 17 + r, :])
            p_e[at, :] = jnp.where(wide == N - 1, 0.0, to_e)
            p_w[at, :] = jnp.where(wide == 0, 0.0, to_w)
            p_n[at, :] = to_n
            p_s[at, :] = to_s
            p_sum[at, :] = to_e + to_w + to_n + to_s + p_u[at, :] + p_d[at, :]

    def beside(ref, it, r):
        return jnp.concatenate([ref[it, c, r : r + 16, :] for c in range(PX)], axis=1).astype(F32)

    def pencil_operator(it, rows, beta):
        edges(it)
        wait_all(rows)
        zp[it, TOP - 1 : TOP, :] = row_recv[it, 0] * has_north
        zp[it, END : END + 1, :] = row_recv[it, 1] * has_south
        for r in range(0, ROWS, 16):
            at = slice(r, r + 16)
            here = zp[it, TOP + r : TOP + r + 16, :]
            out = p_sum[at, :] * here - p_e[at, :] * pltpu.roll(here, N - 1, 1)
            out = out - p_w[at, :] * pltpu.roll(here, 1, 1)
            out = out - p_n[at, :] * zp[it, TOP - 1 + r : TOP + 15 + r, :]
            inner[at, :] = out - p_s[at, :] * zp[it, TOP + 1 + r : TOP + 17 + r, :]
        ratio = None if beta is None else beta()
        await_bytes(above.at[it], line_recv.at[it, 2])
        await_bytes(below.at[it], line_recv.at[it, 3])
        if it == 1:
            to_grid(it)
        sums = jnp.zeros((8, 128), F32)
        for r in range(0, ROWS, 16):
            at = slice(r, r + 16)
            here = zp[it, TOP + r : TOP + r + 16, :]
            out = inner[at, :] - p_u[at, :] * beside(above, it, r) - p_d[at, :] * beside(below, it, r)
            if it == 0:
                image_0[at, :] = out
                lhs[at, :] = out.astype(BF16)
            else:
                here = here + ratio * zp[0, TOP + r : TOP + r + 16, :]
                out = out + ratio * image_0[at, :]
            sums = sums + fold(here * out)
        return sums

    def reduce_start(a, first, second_part):
        mine = jnp.concatenate(
            [first.sum(0, keepdims=True), second_part.sum(0, keepdims=True)], axis=1
        )
        ary_send[a, 0] = mine
        ary[a, q] = mine

        @pl.loop(1, PY)
        def _(t):
            dest = lax.rem(q + t, PY)
            remote(
                ary_send.at[a, 0], ary.at[a, q], ar_send.at[a, 1], ar_recv.at[a, 1], {"py": dest}
            ).start()

        sent_later(ary.at[a, pl.ds(0, PY - 1)], ar_send.at[a, 1])

    def reduce_middle(a):
        await_bytes(ary.at[a, pl.ds(0, PY - 1)], ar_recv.at[a, 1])
        mine = ary[a, 0]
        for t in range(1, PY):
            mine = mine + ary[a, t]
        arx_send[a, 0] = mine
        arx[a, p] = mine
        for t in far:
            dest = lax.rem(p + t, PX)
            remote(
                arx_send.at[a, 0], arx.at[a, p], ar_send.at[a, 0], ar_recv.at[a, 0], {"px": dest}
            ).start()
        sent_later(arx.at[a, pl.ds(0, PX - 1)], ar_send.at[a, 0])

    def reduce_end(a):
        await_bytes(arx.at[a, pl.ds(0, PX - 1)], ar_recv.at[a, 0])
        total = arx[a, 0]
        for t in range(1, PX):
            total = total + arx[a, t]
        return (
            total[:, :128].sum(1, keepdims=True),
            total[:, 128:].sum(1, keepdims=True),
        )

    zero = jnp.zeros((8, 128), F32)

    place_r, place_l = row((8, XL)), lane((8, XL))
    outside = jnp.where(
        ((place_r == 0) & (place_l == 0)) | ((place_r == 1) & (place_l == XL - 1)), 1.0, 0.0
    )

    def grid_direction(it, vp, beta):
        def mixed(ref, k):
            return ref[0, k] if it == 0 else ref[1, k] + beta * ref[0, k]

        for k in range(NZ):
            around = mixed(hrow_recv, k)
            vp[k, TOP - 1 : TOP, :] = around[0]
            vp[k, END : END + 1, :] = around[1]
            halo[k] = lax.dot_general(
                mixed(edge_recv, k), outside, TN, precision=HIGH, preferred_element_type=F32
            )

        @pl.loop(0, NZ)
        def _(k):
            value = brecv[it, k].astype(F32)
            if it == 1:
                value = value + beta * vp_0[k, TOP:END, :]
                direction[k] = value
            vp[k, TOP:END, :] = value

    x_forward(0)
    send_classes()
    gamma_part = spectral(0, None)
    y_back(0)
    coeff_rows = pencil_coefficients()
    rows = x_back(0)
    pencil_weights(coeff_rows)
    curve = pencil_operator(0, rows, None)
    reduce_start(0, gamma_part, curve)

    x_forward(1)
    reduce_middle(0)
    to_grid(0)
    known = []

    def first_alpha():
        if not known:
            gamma, curve = reduce_end(0)
            known.extend([gamma, gamma / curve])
        return known[1]

    reduce_start(1, spectral(1, first_alpha), zero)
    gamma0, alpha0 = known
    y_back(1)
    grid_arrive(0)
    reduce_middle(1)
    grid_direction(0, vp_0, None)

    @pl.loop(0, NZ)
    def _(k):
        res[k] = res[k] - alpha0 * operator(vp_0, k)
        sol[k] = vp_x[k, TOP:END, :] + alpha0 * vp_0[k, TOP:END, :]

    store_x = pltpu.make_async_copy(sol, sol_hbm, store_sem.at[0])
    store_r = pltpu.make_async_copy(res, res_hbm, store_sem.at[1])
    store_x.start()
    store_r.start()
    rows = x_back(1)

    def second_ratio():
        gamma, _ = reduce_end(1)
        known.extend([gamma, gamma / gamma0])
        return known[3]

    reduce_start(2, pencil_operator(1, rows, second_ratio), zero)
    gamma1, beta = known[2:]

    reduce_middle(2)
    grid_arrive(1)
    grid_direction(1, vp_1, beta)
    store_d = pltpu.make_async_copy(direction, dir_hbm, store_sem.at[2])
    store_d.start()

    @pl.loop(0, NZ)
    def _(k):
        image[k] = operator(vp_1, k)

    store_i = pltpu.make_async_copy(image, image_hbm, store_sem.at[3])
    store_i.start()
    curve1, _ = reduce_end(2)
    alpha_out[...] = jnp.broadcast_to(gamma1 / curve1, (1, 128))
    store_a = pltpu.make_async_copy(alpha_out, alpha_hbm, store_sem.at[4])
    store_a.start()

    for wait in pending:
        wait()
    store_x.wait()
    store_r.wait()
    store_d.wait()
    store_i.wait()
    store_a.wait()


def last_update(alpha, x, r, d, image, sol, res, direction, av, xv, rv, dv, iv, load, store):
    loads = [
        pltpu.make_async_copy(src, dst, load.at[i])
        for i, (src, dst) in enumerate(((alpha, av), (d, dv), (x, xv), (image, iv), (r, rv)))
    ]
    for copy in loads:
        copy.start()
    for copy in loads[:2]:
        copy.wait()
    stores = [pltpu.make_async_copy(dv, direction, store.at[0])]
    stores[0].start()
    step = av[0:1, 0:1]
    loads[2].wait()
    xv[...] = xv[...] + step * dv[...]
    stores.append(pltpu.make_async_copy(xv, sol, store.at[1]))
    stores[1].start()
    loads[3].wait()
    loads[4].wait()
    rv[...] = rv[...] - step * iv[...]
    stores.append(pltpu.make_async_copy(rv, res, store.at[2]))
    stores[2].start()
    for copy in stores:
        copy.wait()


def shards(PX, PY, right_side, solution_in, classes, coeff_table, eigenvectors, eigenvalues, level_shift):
    XL, N = right_side.shape[2], eigenvectors.shape[0]
    out = jax.ShapeDtypeStruct(right_side.shape, F32)
    hbm = pl.BlockSpec(memory_space=pl.ANY)
    buffers = scratch(PX, PY, XL, N)
    x, r, d, image, alpha = pl.pallas_call(
        functools.partial(kernel, PX, PY, tuple(buffers)),
        out_shape=[out] * 4 + [jax.ShapeDtypeStruct((1, 128), F32)],
        in_specs=[hbm] * 7,
        out_specs=[hbm] * 5,
        scratch_shapes=list(buffers.values()),
        compiler_params=pltpu.CompilerParams(
            collective_id=0, has_side_effects=True, vmem_limit_bytes=60 * 2**20
        ),
    )(
        right_side,
        solution_in,
        classes,
        coeff_table,
        eigenvectors,
        eigenvalues.reshape(1, N),
        level_shift,
    )
    field = pltpu.VMEM(out.shape, F32)
    return tuple(
        pl.pallas_call(
            last_update,
            out_shape=[out] * 3,
            in_specs=[hbm] * 5,
            out_specs=[hbm] * 3,
            scratch_shapes=[pltpu.VMEM((1, 128), F32)]
            + [field] * 4
            + [pltpu.SemaphoreType.DMA((5,)), pltpu.SemaphoreType.DMA((3,))],
            compiler_params=pltpu.CompilerParams(vmem_limit_bytes=60 * 2**20),
        )(alpha, x, r, d, image)
    )


def solution(mesh):
    field = P(None, "py", "px")
    return jax.shard_map(
        functools.partial(shards, mesh.shape["px"], mesh.shape["py"]),
        mesh=mesh,
        in_specs=(field, field, field, P(), P(), P(), P()),
        out_specs=(field, field, field),
        check_vma=False,
    )
```

```python
import functools

import jax
import jax.numpy as jnp
from jax import lax
from jax.experimental import pallas as pl
from jax.experimental.pallas import tpu as pltpu
from jax.sharding import PartitionSpec as P

F32 = jnp.float32
BF16 = jnp.bfloat16
ROWS = 64
TOP, END = 8, 8 + ROWS
HIGH = lax.Precision.HIGHEST
NT = (((1,), (1,)), ((), ()))
TN = (((0,), (0,)), ((), ()))


def scratch(PX, PY, XL, N):
    NZ = PX
    field = pltpu.VMEM((NZ, ROWS, XL), F32)
    padded = pltpu.VMEM((NZ, ROWS + 16, XL), F32)
    lines = pltpu.VMEM((ROWS, N), F32)
    padded_lines = pltpu.VMEM((ROWS + 16, N), F32)
    tiles = pltpu.VMEM((2, PY, 32, 128), BF16)
    dma = pltpu.SemaphoreType.DMA
    return dict(
        vec=pltpu.VMEM((N, N), BF16),
        eig=pltpu.VMEM((1, N), F32),
        table=pltpu.SMEM((16,), F32),
        shift=pltpu.SMEM((NZ,), F32),
        cls=pltpu.VMEM((NZ, ROWS, XL), jnp.int32),
        sol=field,
        res=field,
        direction=field,
        image=field,
        vp_x=padded,
        vp_0=padded,
        vp_1=padded,
        cp=padded,
        halo=field,
        chalo=field,
        w_e=field,
        w_w=field,
        w_s=field,
        w_n=field,
        w_z=pltpu.VMEM((NZ + 1, ROWS, XL), F32),
        w_sum=field,
        cls_send=pltpu.VMEM((NZ, ROWS, XL), BF16),
        cls_recv=pltpu.VMEM((3, PX, ROWS, XL), BF16),
        pc=padded_lines,
        p_e=lines,
        p_w=lines,
        p_s=lines,
        p_n=lines,
        p_u=lines,
        p_d=lines,
        p_sum=lines,
        zp=pltpu.VMEM((2, ROWS + 16, N), F32),
        above=pltpu.VMEM((2, PX, ROWS, XL), BF16),
        below=pltpu.VMEM((2, PX, ROWS, XL), BF16),
        row_send=pltpu.VMEM((3, 2, 1, N), F32),
        row_recv=pltpu.VMEM((3, 2, 1, N), F32),
        xsend=pltpu.VMEM((PX, ROWS, XL), BF16),
        xrecv=pltpu.VMEM((PX, ROWS, XL), BF16),
        ysend=tiles,
        yrecv=tiles,
        zsend=tiles,
        zrecv=tiles,
        bsend=pltpu.VMEM((2, PX, ROWS, XL), BF16),
        brecv=pltpu.VMEM((2, PX, ROWS, XL), BF16),
        lhs=pltpu.VMEM((ROWS, N), BF16),
        acc=lines,
        inner=lines,
        image_0=lines,
        s2=lines,
        s3=pltpu.VMEM((ROWS, N), BF16),
        dinv=lines,
        eigc=pltpu.VMEM((128, 128), F32),
        rsend=pltpu.VMEM((1, 2, 2 * NZ, XL), F32),
        rrecv=pltpu.VMEM((1, 2, 2 * NZ, XL), F32),
        csend=pltpu.VMEM((1, 8, NZ * ROWS), F32),
        crecv=pltpu.VMEM((1, 16, NZ * ROWS), F32),
        hrow_send=pltpu.VMEM((2, PX, 2, 1, XL), F32),
        hrow_recv=pltpu.VMEM((2, PX, 2, 1, XL), F32),
        edge_send=pltpu.VMEM((2, PX, 8, ROWS), F32),
        edge_recv=pltpu.VMEM((2, PX, 8, ROWS), F32),
        alpha_out=pltpu.VMEM((1, 128), F32),
        arx_send=pltpu.VMEM((3, 1, 1, 256), F32),
        arx=pltpu.VMEM((3, PX, 1, 256), F32),
        ary_send=pltpu.VMEM((3, 1, 1, 256), F32),
        ary=pltpu.VMEM((3, PY, 1, 256), F32),
        load_sem=dma((7,)),
        store_sem=dma((5,)),
        halo_send=dma((1, 4)),
        halo_recv=dma((1, 4)),
        grid_send=dma((2, 2)),
        grid_recv=dma((2, 2)),
        cls_sem=dma((2, 3)),
        line_send=dma((3, 4)),
        line_recv=dma((3, 4)),
        a2a_send=dma((2, 4)),
        a2a_recv=dma((2, 4, 8)),
        ar_send=dma((3, 2)),
        ar_recv=dma((3, 2)),
    )


def kernel(PX, PY, names, *refs):
    b_hbm, x_hbm, cls_hbm, table_hbm, vec_hbm, eig_hbm, shift_hbm = refs[:7]
    sol_hbm, res_hbm, dir_hbm, image_hbm, alpha_hbm = refs[7:12]
    R = dict(zip(names, refs[12:]))
    vec, eig, table, shift, cls = (R[n] for n in ("vec", "eig", "table", "shift", "cls"))
    sol, res, direction, image = (R[n] for n in ("sol", "res", "direction", "image"))
    vp_x, vp_0, vp_1, cp, halo, chalo = (R[n] for n in ("vp_x", "vp_0", "vp_1", "cp", "halo", "chalo"))
    w_e, w_w, w_s, w_n, w_z, w_sum = (R[n] for n in ("w_e", "w_w", "w_s", "w_n", "w_z", "w_sum"))
    p_e, p_w, p_s, p_n, p_u, p_d, p_sum = (
        R[n] for n in ("p_e", "p_w", "p_s", "p_n", "p_u", "p_d", "p_sum")
    )
    cls_send, cls_recv, pc, zp = (R[n] for n in ("cls_send", "cls_recv", "pc", "zp"))
    above, below, row_send, row_recv = (R[n] for n in ("above", "below", "row_send", "row_recv"))
    xsend, xrecv, ysend, yrecv = (R[n] for n in ("xsend", "xrecv", "ysend", "yrecv"))
    zsend, zrecv, bsend, brecv = (R[n] for n in ("zsend", "zrecv", "bsend", "brecv"))
    lhs, s2, s3, dinv, eigc = (R[n] for n in ("lhs", "s2", "s3", "dinv", "eigc"))
    acc, inner, image_0 = (R[n] for n in ("acc", "inner", "image_0"))
    rsend, rrecv, csend, crecv = (R[n] for n in ("rsend", "rrecv", "csend", "crecv"))
    hrow_send, hrow_recv, edge_send, edge_recv, grid_send, grid_recv, alpha_out = (
        R[n]
        for n in (
            "hrow_send",
            "hrow_recv",
            "edge_send",
            "edge_recv",
            "grid_send",
            "grid_recv",
            "alpha_out",
        )
    )
    arx_send, arx, ary_send, ary = (R[n] for n in ("arx_send", "arx", "ary_send", "ary"))
    load_sem, store_sem, halo_send, halo_recv = (
        R[n] for n in ("load_sem", "store_sem", "halo_send", "halo_recv")
    )
    cls_sem, line_send, line_recv = (R[n] for n in ("cls_sem", "line_send", "line_recv"))
    a2a_send, a2a_recv, ar_send, ar_recv = (
        R[n] for n in ("a2a_send", "a2a_recv", "ar_send", "ar_recv")
    )

    NZ, XL, N = PX, image.shape[2], vec.shape[0]
    G = N // 256
    p, q = lax.axis_index("px"), lax.axis_index("py")
    pending = []
    far = sorted(range(1, PX), key=lambda t: -min(t, PX - t))
    far_groups = sorted(range(G), key=lambda t: -min(t, G - t))

    def lane(shape):
        return lax.broadcasted_iota(jnp.int32, shape, len(shape) - 1)

    def row(shape):
        return lax.broadcasted_iota(jnp.int32, shape, len(shape) - 2)

    def block(i, size):
        return pl.ds(pl.multiple_of(i * size, size), size)

    def remote(src, dst, send, recv, where):
        return pltpu.make_async_remote_copy(
            src_ref=src, dst_ref=dst, send_sem=send, recv_sem=recv, device_id=where
        )

    def await_bytes(ref, sem):
        pltpu.make_async_copy(ref, ref, sem).wait()

    def sent_later(ref, sem):
        pending.append(lambda: await_bytes(ref, sem))

    north = {"py": lax.rem(q + PY - 1, PY)}
    south = {"py": lax.rem(q + 1, PY)}
    west_of = {"px": lax.rem(p + PX - 1, PX)}
    east_of = {"px": lax.rem(p + 1, PX)}
    has_north = jnp.where(q > 0, 1.0, 0.0).astype(F32)
    has_south = jnp.where(q < PY - 1, 1.0, 0.0).astype(F32)
    has_first = jnp.where(p > 0, 1.0, 0.0).astype(F32)
    has_last = jnp.where(p < PX - 1, 1.0, 0.0).astype(F32)

    load_cls = pltpu.make_async_copy(cls_hbm, cls, load_sem.at[0])
    load_x = pltpu.make_async_copy(x_hbm, vp_x.at[:, TOP:END, :], load_sem.at[1])
    load_b = pltpu.make_async_copy(b_hbm, res, load_sem.at[2])
    load_v = pltpu.make_async_copy(vec_hbm, vec, load_sem.at[3])
    load_t = pltpu.make_async_copy(table_hbm, table, load_sem.at[4])
    load_s = pltpu.make_async_copy(shift_hbm, shift, load_sem.at[5])
    load_e = pltpu.make_async_copy(eig_hbm, eig, load_sem.at[6])
    for load in (load_x, load_cls, load_t, load_s, load_e, load_b, load_v):
        load.start()

    barrier = pltpu.get_barrier_semaphore()

    @pl.loop(1, PX)
    def _(t):
        pl.semaphore_signal(barrier, inc=1, device_id={"px": lax.rem(p + t, PX)})

    @pl.loop(1, PY)
    def _(t):
        pl.semaphore_signal(barrier, inc=1, device_id={"py": lax.rem(q + t, PY)})

    def pick(base, kind, rows):
        r, l = row((rows, XL)), lane((rows, XL))
        hot = ((r == base) & (l == 0)) | ((r == base + 1) & (l == XL - 1))
        return jnp.where(hot, 1.0, 0.0).astype(kind)

    def place(base):
        r, l = row((16, XL)), lane((16, XL))
        hot_l = jnp.where((r == base + 1) & (l == 0), has_first, 0.0)
        hot_r = jnp.where((r == 8 + base) & (l == XL - 1), has_last, 0.0)
        return hot_l + hot_r

    def lookup(values):
        picks = values.astype(jnp.int32)
        level = [table[label] for label in range(16)]
        for bit in range(4):
            odd = (picks & (1 << bit)) != 0
            level = [jnp.where(odd, level[i + 1], level[i]) for i in range(0, len(level), 2)]
        return level[0]

    def halo_copies(h):
        return [
            remote(rsend.at[h, 0], rrecv.at[h, 1], halo_send.at[h, 0], halo_recv.at[h, 0], north),
            remote(rsend.at[h, 1], rrecv.at[h, 0], halo_send.at[h, 1], halo_recv.at[h, 1], south),
            remote(csend.at[h], crecv.at[h, pl.ds(8, 8)], halo_send.at[h, 2], halo_recv.at[h, 2], west_of),
            remote(csend.at[h], crecv.at[h, pl.ds(0, 8)], halo_send.at[h, 3], halo_recv.at[h, 3], east_of),
        ]

    def start(copies):
        for copy in copies:
            copy.start()
            pending.append(copy.wait_send)
        return copies

    load_x.wait()
    load_cls.wait()
    for k in range(NZ):
        rsend[0, 0, k : k + 1, :] = vp_x[k, TOP : TOP + 1, :]
        rsend[0, 1, k : k + 1, :] = vp_x[k, END - 1 : END, :]
        rsend[0, 0, NZ + k : NZ + k + 1, :] = cls[k, 0:1, :].astype(F32)
        rsend[0, 1, NZ + k : NZ + k + 1, :] = cls[k, ROWS - 1 : ROWS, :].astype(F32)
    x_flat = vp_x[:, TOP:END, :].reshape(NZ * ROWS, XL)
    cls_flat = cls[...].reshape(NZ * ROWS, XL).astype(F32).astype(BF16)
    csend[0] = (
        lax.dot_general(pick(0, BF16, 16), x_flat.astype(BF16), NT, preferred_element_type=F32)
        + lax.dot_general(pick(2, BF16, 16), cls_flat, NT, preferred_element_type=F32)
    )[0:8]
    cls_send[...] = cls_flat.reshape(NZ, ROWS, XL)
    load_t.wait()
    load_s.wait()
    load_e.wait()
    pl.semaphore_wait(barrier, PX - 1 + PY - 1)
    copies = start(halo_copies(0))

    @pl.loop(0, NZ)
    def _(k):
        cp[k, TOP:END, :] = lookup(cls[k])

    w_z[0] = jnp.zeros((ROWS, XL), F32)
    w_z[NZ] = jnp.zeros((ROWS, XL), F32)

    @pl.loop(0, NZ - 1)
    def _(k):
        w_z[k + 1] = 0.5 * (cp[k, TOP:END, :] + cp[k + 1, TOP:END, :])

    def wait_all(copies):
        for copy in copies:
            copy.wait_recv()

    def fill_rows(h, vp):
        for k in range(NZ):
            vp[k, TOP - 1 : TOP, :] = rrecv[h, 0, k : k + 1, :] * has_north
            vp[k, END : END + 1, :] = rrecv[h, 1, k : k + 1, :] * has_south

    wait_all(copies)
    fill_rows(0, vp_x)
    north_row = lookup(rrecv[0, 0, NZ : 2 * NZ, :]) * has_north
    south_row = lookup(rrecv[0, 1, NZ : 2 * NZ, :]) * has_south
    for k in range(NZ):
        cp[k, TOP - 1 : TOP, :] = north_row[k : k + 1]
        cp[k, END : END + 1, :] = south_row[k : k + 1]

    def columns(values, base):
        high = values.astype(BF16)
        rest = values - high.astype(F32)
        middle = rest.astype(BF16)
        low = (rest - middle.astype(F32)).astype(BF16)
        hot = place(base).astype(BF16)
        out = lax.dot_general(
            jnp.concatenate([high, middle, low], axis=0),
            jnp.concatenate([hot, hot, hot], axis=0),
            TN,
            preferred_element_type=F32,
        )
        return out.reshape(NZ, ROWS, XL)

    halo[...] = columns(crecv[0], 0)
    chalo[...] = columns(lookup(crecv[0]), 2)

    lanes = lane((ROWS, XL))

    def east(values, edge):
        return jnp.where(lanes == XL - 1, edge, pltpu.roll(values, XL - 1, 1))

    def west(values, edge):
        return jnp.where(lanes == 0, edge, pltpu.roll(values, 1, 1))

    def weights(k):
        here = cp[k, TOP:END, :]
        edge = chalo[k]
        to_e = 0.5 * (here + east(here, edge))
        to_w = 0.5 * (here + west(here, edge))
        to_n = 0.5 * (here + cp[k, TOP - 1 : END - 1, :])
        to_s = 0.5 * (here + cp[k, TOP + 1 : END + 1, :])
        w_e[k] = to_e
        w_w[k] = to_w
        w_n[k] = to_n
        w_s[k] = to_s
        w_sum[k] = to_e + to_w + to_n + to_s + w_z[k] + w_z[k + 1]

    def operator(vp, k):
        here = vp[k, TOP:END, :]
        edge = halo[k]
        lower = vp[jnp.maximum(k - 1, 0), TOP:END, :]
        upper = vp[jnp.minimum(k + 1, NZ - 1), TOP:END, :]
        out = w_sum[k] * here - w_e[k] * east(here, edge) - w_w[k] * west(here, edge)
        out = out - w_n[k] * vp[k, TOP - 1 : END - 1, :] - w_s[k] * vp[k, TOP + 1 : END + 1, :]
        return out - w_z[k] * lower - w_z[k + 1] * upper

    def fold(values):
        part = values.reshape(values.shape[0] // 8, 8, values.shape[1]).sum(0)
        out = part[:, :128]
        for c in range(128, values.shape[1], 128):
            out = out + part[:, c : c + 128]
        return out

    load_b.wait()
    for t in far + [0]:
        k = lax.rem(p + t, NZ)
        weights(k)
        value = res[k] - operator(vp_x, k)
        res[k] = value
        if t:
            xsend[k] = value.astype(BF16)
            remote(
                xsend.at[k], xrecv.at[p], a2a_send.at[0, 0], a2a_recv.at[0, 0, p], {"px": k}
            ).start()
        else:
            xrecv[p] = value.astype(BF16)
    sent_later(xsend.at[pl.ds(0, PX - 1)], a2a_send.at[0, 0])

    group, part = q // 4, lax.rem(q, 4)
    for half in range(2):
        cols = pl.ds(pl.multiple_of(group * 256 + half * 128, 128), 128)
        eigc[...] = jnp.broadcast_to(eig[:, cols], (128, 128)).T
        mine = eigc[block(part, 32), 0:1] + shift[p]
        dinv[half * 32 : half * 32 + 32, :] = 1.0 / (mine + eig[...])

    load_v.wait()

    half_lane = lane((32, 128)) < 64
    own_group = q // 4

    def product(ref, rows, cols):
        return jnp.dot(ref[:, rows], vec[rows, cols], preferred_element_type=F32)

    def in_steps(parts, size, fetch, consume, order):
        steps = [parts[i : i + 2] for i in range(0, len(parts), 2)]
        for i, step in enumerate(steps):
            rows = [block(fetch(t), size) for t in step]
            for n in order:
                cols = block(n, 256)
                tile = product(lhs, rows[0], cols)
                for r in rows[1:]:
                    tile = tile + product(lhs, r, cols)
                if i:
                    tile = acc[:, cols] + tile
                if i == len(steps) - 1:
                    consume(n, tile)
                else:
                    acc[:, cols] = tile

    def scatter_tile(src, dst, it, which, t, g):
        for u in range(4):
            if t == 0 and u == 0:
                dst[it, q] = src[it, q]
                continue
            dest = g * 4 + (lax.rem(q + u, 4) if t == 0 else u)
            remote(
                src.at[it, dest],
                dst.at[it, q],
                a2a_send.at[it, which],
                a2a_recv.at[it, which, own_group],
                {"py": dest},
            ).start()

    def await_group(dst, it, which, t):
        g = lax.rem(own_group + G - t, G)
        await_bytes(dst.at[it, pl.ds(0, 4 if t else 3)], a2a_recv.at[it, which, g])
        return g

    groups = [lax.rem(own_group + t, G) for t in far_groups]

    def fetch_x(t):
        c = lax.rem(p + PX - t, PX)
        if t:
            await_bytes(xrecv.at[0], a2a_recv.at[0, 0, c])
        lhs[:, block(c, XL)] = xrecv[c]
        return c

    def x_forward(it):
        def turn(i, g, tile):
            turned = jnp.concatenate([tile[:, :128], tile[:, 128:]], axis=0).T
            ysend[it, block(g, 4)] = turned.astype(BF16).reshape(4, 32, 128)
            scatter_tile(ysend, yrecv, it, 1, far_groups[i], g)

        if it == 0:
            count = iter(range(G))
            in_steps([0] + far, XL, fetch_x, lambda g, tile: turn(next(count), g, tile), groups)
        else:
            for i, g in enumerate(groups):
                turn(i, g, product(lhs, slice(None), block(g, 256)))
        sent_later(ysend.at[it, pl.ds(0, PY - 1)], a2a_send.at[it, 1])

    def fetch_y(it):
        def fetch(t):
            g = await_group(yrecv, it, 1, t)
            for m in range(2):
                even = yrecv[it, 4 * g + 2 * m].astype(F32)
                odd = yrecv[it, 4 * g + 2 * m + 1].astype(F32)
                low = jnp.where(half_lane, even, pltpu.roll(odd, 64, 1))
                high = jnp.where(half_lane, pltpu.roll(even, 64, 1), odd)
                cols = block(2 * g + m, 128)
                lhs[0:32, cols] = low.astype(BF16)
                lhs[32:64, cols] = high.astype(BF16)
            return g

        return fetch

    def spectral(it, alpha):
        sums = []

        def scale(n, tile):
            cols = block(n, 256)
            scaled = (tile * dinv[:, cols]).astype(BF16)
            s3[:, cols] = scaled
            sums.append(fold(tile * scaled.astype(F32)))

        def keep(n, tile):
            cols = block(n, 256)
            if it == 0:
                s2[:, cols] = tile
                scale(n, tile)
            else:
                acc[:, cols] = tile

        in_steps(far_groups, 256, fetch_y(it), keep, range(G))
        if it == 1:
            step = alpha()
            for n in range(G):
                cols = block(n, 256)
                scale(n, s2[:, cols] - step * acc[:, cols])
        return sum(sums[1:], sums[0])

    def y_back(it):
        for i, g in enumerate(groups):
            tile = product(s3, slice(None), block(g, 256))
            for h in range(2):
                low, high = tile[0:32, h * 128 : h * 128 + 128], tile[32:64, h * 128 : h * 128 + 128]
                even = jnp.where(half_lane, low, pltpu.roll(high, 64, 1))
                odd = jnp.where(half_lane, pltpu.roll(low, 64, 1), high)
                zsend[it, g * 4 + 2 * h] = even.astype(BF16)
                zsend[it, g * 4 + 2 * h + 1] = odd.astype(BF16)
            scatter_tile(zsend, zrecv, it, 2, far_groups[i], g)
        sent_later(zsend.at[it, pl.ds(0, PY - 1)], a2a_send.at[it, 2])

    def fetch_z(it):
        def fetch(t):
            g = await_group(zrecv, it, 2, t)
            turned = zrecv[it, block(g, 4)].reshape(128, 128).astype(F32).T.astype(BF16)
            lhs[:, block(2 * g, 128)] = turned[0:64]
            lhs[:, block(2 * g + 1, 128)] = turned[64:128]
            return g

        return fetch

    def line_copies(h):
        return [
            remote(row_send.at[h, 0], row_recv.at[h, 1], line_send.at[h, 0], line_recv.at[h, 0], north),
            remote(row_send.at[h, 1], row_recv.at[h, 0], line_send.at[h, 1], line_recv.at[h, 1], south),
        ]

    def x_back(it):
        def spread(n, tile):
            for c in range(n * 256 // XL, (n + 1) * 256 // XL):
                part = tile[:, c * XL - n * 256 : (c + 1) * XL - n * 256].astype(BF16)
                bsend[it, c] = part
                zp[it, TOP:END, c * XL : (c + 1) * XL] = part.astype(F32)
                for dst, i, where in ((above, 2, west_of), (below, 3, east_of)):
                    remote(
                        bsend.at[it, c], dst.at[it, c], line_send.at[it, i], line_recv.at[it, i], where
                    ).start()

        in_steps(far_groups, 256, fetch_z(it), spread, range(G))
        row_send[it, 0] = zp[it, TOP : TOP + 1, :]
        row_send[it, 1] = zp[it, END - 1 : END, :]
        rows = start(line_copies(it))
        sent_later(bsend.at[it], line_send.at[it, 2])
        sent_later(bsend.at[it], line_send.at[it, 3])
        return rows

    def edges(it):
        r, l = row((8 * PX, XL)), lane((8 * PX, XL))
        out = jnp.zeros((8 * PX, ROWS), F32)
        for c in range(PX):
            hot = ((r == 8 * c + 8) & (l == XL - 1)) | ((r == 8 * c - 7) & (l == 0))
            out = out + lax.dot_general(
                jnp.where(hot, 1.0, 0.0).astype(BF16), bsend[it, c], NT, preferred_element_type=F32
            )
        edge_send[it] = out.reshape(PX, 8, ROWS)

    def to_grid(it):
        for c in range(PX):
            cols = slice(c * XL, (c + 1) * XL)
            hrow_send[it, c, 0] = zp[it, TOP - 1 : TOP, cols]
            hrow_send[it, c, 1] = zp[it, END : END + 1, cols]
        trio = (
            (bsend, brecv, a2a_send.at[it, 3], a2a_recv.at[it, 3, 0]),
            (hrow_send, hrow_recv, grid_send.at[it, 0], grid_recv.at[it, 0]),
            (edge_send, edge_recv, grid_send.at[it, 1], grid_recv.at[it, 1]),
        )
        for t in far:
            c = lax.rem(p + t, PX)
            for src, dst, send, recv in trio:
                remote(src.at[it, c], dst.at[it, p], send, recv, {"px": c}).start()
        for src, dst, send, recv in trio:
            dst[it, p] = src[it, p]
            sent_later(src.at[it, pl.ds(0, PX - 1)], send)

    def grid_arrive(it):
        for dst, recv in (
            (brecv, a2a_recv.at[it, 3, 0]),
            (hrow_recv, grid_recv.at[it, 0]),
            (edge_recv, grid_recv.at[it, 1]),
        ):
            await_bytes(dst.at[it, pl.ds(0, PX - 1)], recv)

    def plane_copies():
        return [
            remote(cls_recv.at[1], cls_recv.at[2], cls_sem.at[0, 2], cls_sem.at[1, 2], west_of),
            remote(cls_recv.at[1], cls_recv.at[0], cls_sem.at[0, 0], cls_sem.at[1, 0], east_of),
        ]

    def send_classes():
        for t in far:
            k = lax.rem(p + t, PX)
            remote(
                cls_send.at[k], cls_recv.at[1, p], cls_sem.at[0, 1], cls_sem.at[1, 1], {"px": k}
            ).start()
        cls_recv[1, p] = cls_send[p]
        sent_later(cls_recv.at[1, pl.ds(0, PX - 1)], cls_sem.at[0, 1])

    def pencil_coefficients():
        await_bytes(cls_recv.at[1, pl.ds(0, PX - 1)], cls_sem.at[1, 1])
        planes = start(plane_copies())

        @pl.loop(0, PX)
        def _(c):
            pc[TOP:END, block(c, XL)] = lookup(cls_recv[1, c].astype(F32))

        row_send[2, 0] = pc[TOP : TOP + 1, :]
        row_send[2, 1] = pc[END - 1 : END, :]
        return planes + start(line_copies(2))

    wide = lane((16, N))

    def pencil_weights(rows):
        wait_all(rows)

        @pl.loop(0, PX)
        def _(c):
            cols = block(c, XL)
            here = pc[TOP:END, cols]
            p_d[:, cols] = 0.5 * has_first * (here + lookup(cls_recv[0, c].astype(F32)))
            p_u[:, cols] = 0.5 * has_last * (here + lookup(cls_recv[2, c].astype(F32)))

        pc[TOP - 1 : TOP, :] = row_recv[2, 0] * has_north
        pc[END : END + 1, :] = row_recv[2, 1] * has_south
        for r in range(0, ROWS, 16):
            at = slice(r, r + 16)
            here = pc[TOP + r : TOP + r + 16, :]
            to_e = 0.5 * (here + jnp.where(wide == N - 1, 0.0, pltpu.roll(here, N - 1, 1)))
            to_w = 0.5 * (here + jnp.where(wide == 0, 0.0, pltpu.roll(here, 1, 1)))
            to_n = 0.5 * (here + pc[TOP - 1 + r : TOP + 15 + r, :])
            to_s = 0.5 * (here + pc[TOP + 1 + r : TOP + 17 + r, :])
            p_e[at, :] = jnp.where(wide == N - 1, 0.0, to_e)
            p_w[at, :] = jnp.where(wide == 0, 0.0, to_w)
            p_n[at, :] = to_n
            p_s[at, :] = to_s
            p_sum[at, :] = to_e + to_w + to_n + to_s + p_u[at, :] + p_d[at, :]

    def beside(ref, it, r):
        return jnp.concatenate([ref[it, c, r : r + 16, :] for c in range(PX)], axis=1).astype(F32)

    def pencil_operator(it, rows, beta):
        edges(it)
        wait_all(rows)
        zp[it, TOP - 1 : TOP, :] = row_recv[it, 0] * has_north
        zp[it, END : END + 1, :] = row_recv[it, 1] * has_south
        for r in range(0, ROWS, 16):
            at = slice(r, r + 16)
            here = zp[it, TOP + r : TOP + r + 16, :]
            out = p_sum[at, :] * here - p_e[at, :] * pltpu.roll(here, N - 1, 1)
            out = out - p_w[at, :] * pltpu.roll(here, 1, 1)
            out = out - p_n[at, :] * zp[it, TOP - 1 + r : TOP + 15 + r, :]
            inner[at, :] = out - p_s[at, :] * zp[it, TOP + 1 + r : TOP + 17 + r, :]
        ratio = None if beta is None else beta()
        await_bytes(above.at[it], line_recv.at[it, 2])
        await_bytes(below.at[it], line_recv.at[it, 3])
        if it == 1:
            to_grid(it)
        sums = jnp.zeros((8, 128), F32)
        for r in range(0, ROWS, 16):
            at = slice(r, r + 16)
            here = zp[it, TOP + r : TOP + r + 16, :]
            out = inner[at, :] - p_u[at, :] * beside(above, it, r) - p_d[at, :] * beside(below, it, r)
            if it == 0:
                image_0[at, :] = out
                lhs[at, :] = out.astype(BF16)
            else:
                here = here + ratio * zp[0, TOP + r : TOP + r + 16, :]
                out = out + ratio * image_0[at, :]
            sums = sums + fold(here * out)
        return sums

    def reduce_start(a, first, second_part):
        mine = jnp.concatenate(
            [first.sum(0, keepdims=True), second_part.sum(0, keepdims=True)], axis=1
        )
        ary_send[a, 0] = mine
        ary[a, q] = mine

        @pl.loop(1, PY)
        def _(t):
            dest = lax.rem(q + t, PY)
            remote(
                ary_send.at[a, 0], ary.at[a, q], ar_send.at[a, 1], ar_recv.at[a, 1], {"py": dest}
            ).start()

        sent_later(ary.at[a, pl.ds(0, PY - 1)], ar_send.at[a, 1])

    def reduce_middle(a):
        await_bytes(ary.at[a, pl.ds(0, PY - 1)], ar_recv.at[a, 1])
        mine = ary[a, 0]
        for t in range(1, PY):
            mine = mine + ary[a, t]
        arx_send[a, 0] = mine
        arx[a, p] = mine
        for t in far:
            dest = lax.rem(p + t, PX)
            remote(
                arx_send.at[a, 0], arx.at[a, p], ar_send.at[a, 0], ar_recv.at[a, 0], {"px": dest}
            ).start()
        sent_later(arx.at[a, pl.ds(0, PX - 1)], ar_send.at[a, 0])

    def reduce_end(a):
        await_bytes(arx.at[a, pl.ds(0, PX - 1)], ar_recv.at[a, 0])
        total = arx[a, 0]
        for t in range(1, PX):
            total = total + arx[a, t]
        return (
            total[:, :128].sum(1, keepdims=True),
            total[:, 128:].sum(1, keepdims=True),
        )

    zero = jnp.zeros((8, 128), F32)

    place_r, place_l = row((8, XL)), lane((8, XL))
    outside = jnp.where(
        ((place_r == 0) & (place_l == 0)) | ((place_r == 1) & (place_l == XL - 1)), 1.0, 0.0
    )

    def grid_direction(it, vp, beta):
        def mixed(ref, k):
            return ref[0, k] if it == 0 else ref[1, k] + beta * ref[0, k]

        for k in range(NZ):
            around = mixed(hrow_recv, k)
            vp[k, TOP - 1 : TOP, :] = around[0]
            vp[k, END : END + 1, :] = around[1]
            halo[k] = lax.dot_general(
                mixed(edge_recv, k), outside, TN, precision=HIGH, preferred_element_type=F32
            )

        @pl.loop(0, NZ)
        def _(k):
            value = brecv[it, k].astype(F32)
            if it == 1:
                value = value + beta * vp_0[k, TOP:END, :]
                direction[k] = value
            vp[k, TOP:END, :] = value

    x_forward(0)
    send_classes()
    gamma_part = spectral(0, None)
    y_back(0)
    coeff_rows = pencil_coefficients()
    rows = x_back(0)
    pencil_weights(coeff_rows)
    curve = pencil_operator(0, rows, None)
    reduce_start(0, gamma_part, curve)

    x_forward(1)
    reduce_middle(0)
    to_grid(0)
    known = []

    def first_alpha():
        if not known:
            gamma, curve = reduce_end(0)
            known.extend([gamma, gamma / curve])
        return known[1]

    reduce_start(1, spectral(1, first_alpha), zero)
    gamma0, alpha0 = known
    y_back(1)
    grid_arrive(0)
    grid_direction(0, vp_0, None)

    @pl.loop(0, NZ)
    def _(k):
        res[k] = res[k] - alpha0 * operator(vp_0, k)
        sol[k] = vp_x[k, TOP:END, :] + alpha0 * vp_0[k, TOP:END, :]

    store_x = pltpu.make_async_copy(sol, sol_hbm, store_sem.at[0])
    store_r = pltpu.make_async_copy(res, res_hbm, store_sem.at[1])
    store_x.start()
    store_r.start()
    reduce_middle(1)
    rows = x_back(1)

    def second_ratio():
        gamma, _ = reduce_end(1)
        known.extend([gamma, gamma / gamma0])
        return known[3]

    reduce_start(2, pencil_operator(1, rows, second_ratio), zero)
    gamma1, beta = known[2:]

    reduce_middle(2)
    grid_arrive(1)
    grid_direction(1, vp_1, beta)
    store_d = pltpu.make_async_copy(direction, dir_hbm, store_sem.at[2])
    store_d.start()

    @pl.loop(0, NZ)
    def _(k):
        image[k] = operator(vp_1, k)

    store_i = pltpu.make_async_copy(image, image_hbm, store_sem.at[3])
    store_i.start()
    curve1, _ = reduce_end(2)
    alpha_out[...] = jnp.broadcast_to(gamma1 / curve1, (1, 128))
    store_a = pltpu.make_async_copy(alpha_out, alpha_hbm, store_sem.at[4])
    store_a.start()

    for wait in pending:
        wait()
    store_x.wait()
    store_r.wait()
    store_d.wait()
    store_i.wait()
    store_a.wait()


def last_update(alpha, x, r, d, image, sol, res, direction, av, xv, rv, dv, iv, load, store):
    loads = [
        pltpu.make_async_copy(src, dst, load.at[i])
        for i, (src, dst) in enumerate(((alpha, av), (d, dv), (x, xv), (image, iv), (r, rv)))
    ]
    for copy in loads:
        copy.start()
    for copy in loads[:2]:
        copy.wait()
    stores = [pltpu.make_async_copy(dv, direction, store.at[0])]
    stores[0].start()
    step = av[0:1, 0:1]
    loads[2].wait()
    xv[...] = xv[...] + step * dv[...]
    stores.append(pltpu.make_async_copy(xv, sol, store.at[1]))
    stores[1].start()
    loads[3].wait()
    loads[4].wait()
    rv[...] = rv[...] - step * iv[...]
    stores.append(pltpu.make_async_copy(rv, res, store.at[2]))
    stores[2].start()
    for copy in stores:
        copy.wait()


def shards(PX, PY, right_side, solution_in, classes, coeff_table, eigenvectors, eigenvalues, level_shift):
    XL, N = right_side.shape[2], eigenvectors.shape[0]
    out = jax.ShapeDtypeStruct(right_side.shape, F32)
    hbm = pl.BlockSpec(memory_space=pl.ANY)
    buffers = scratch(PX, PY, XL, N)
    x, r, d, image, alpha = pl.pallas_call(
        functools.partial(kernel, PX, PY, tuple(buffers)),
        out_shape=[out] * 4 + [jax.ShapeDtypeStruct((1, 128), F32)],
        in_specs=[hbm] * 7,
        out_specs=[hbm] * 5,
        scratch_shapes=list(buffers.values()),
        compiler_params=pltpu.CompilerParams(
            collective_id=0, has_side_effects=True, vmem_limit_bytes=60 * 2**20
        ),
    )(
        right_side,
        solution_in,
        classes,
        coeff_table,
        eigenvectors,
        eigenvalues.reshape(1, N),
        level_shift,
    )
    field = pltpu.VMEM(out.shape, F32)
    return tuple(
        pl.pallas_call(
            last_update,
            out_shape=[out] * 3,
            in_specs=[hbm] * 5,
            out_specs=[hbm] * 3,
            scratch_shapes=[pltpu.VMEM((1, 128), F32)]
            + [field] * 4
            + [pltpu.SemaphoreType.DMA((5,)), pltpu.SemaphoreType.DMA((3,))],
            compiler_params=pltpu.CompilerParams(vmem_limit_bytes=60 * 2**20),
        )(alpha, x, r, d, image)
    )


def solution(mesh):
    field = P(None, "py", "px")
    return jax.shard_map(
        functools.partial(shards, mesh.shape["px"], mesh.shape["py"]),
        mesh=mesh,
        in_specs=(field, field, field, P(), P(), P(), P()),
        out_specs=(field, field, field),
        check_vma=False,
    )
```
